256 devices in a mesh: dp: 8 (over x, core), vocab: 32 (over z, y).
Axes of the slice: x: 4, y: 4, z: 8, core: 2. Of those that a mesh axis runs over, the one named last changes fastest.
Arguments:
- hidden: bfloat16 [1024, 2880], P('dp'), as said below
- ref_hidden: bfloat16 [1024, 2880], P('dp')
- sampled: int32 [1024], P('dp'), may hold values from 0 to 163839
- advantage: float32 [1024], P('dp'), may hold values from -4 to 4
- policy_head: bfloat16 [2880, 163840], P(None, ('dp', 'vocab'))
- ref_head: bfloat16 [2880, 163840], P(None, ('dp', 'vocab'))
Outputs:
- logp: float32 [1024], P('dp')
- entropy: float32 [1024], P('dp')
- kl: float32 [1024], P('dp')
- d_hidden: float32 [1024, 2880], P('dp', 'vocab')
- d_policy: bfloat16 [2880, 163840], P(None, ('dp', 'vocab'))
The draws below stay inside these ranges and needn't reach their ends.
Inputs may be any that keep to these rules, and one draw needn't show every extreme that they name: Weights and hidden states are of order one in the scale of the width; no further structure is promised.
All inputs are finite; a program needn't handle non-finite values.
Results may differ from the reference program's by a relative error of at most 0.0049.
Values may be sent and summed in bfloat16 or wider, within the bound.
No kernel may reach another device: no remote copies, remote signals or barrier semaphores. Data moves between devices by JAX's collectives and lax.ppermute only.
A program may use at most 128 MiB of HBM per device.

```python
import math
import jax
import jax.numpy as jnp

H = 2880
V = 163840
TOKENS = 1024


def head_columns(key, salt):
    key = jax.random.fold_in(key, salt)
    return jax.random.normal(key, (H, V), jnp.float32) * (3.0 / math.sqrt(H))


def draw_policy_head(key, part):
    return head_columns(key, 101).astype(jnp.bfloat16)


def draw_ref_head(key, part):
    return head_columns(key, 202).astype(jnp.bfloat16)


def draw_hidden(key, part):
    key = jax.random.fold_in(key, 7)
    key_base = jax.random.fold_in(key, 0)
    values = jax.random.normal(key_base, (TOKENS, H), jnp.float32)
    return values.astype(jnp.bfloat16)


def draw_ref_hidden(key, part):
    key = jax.random.fold_in(key, 8)
    key_base = jax.random.fold_in(key, 0)
    values = jax.random.normal(key_base, (TOKENS, H), jnp.float32)
    return values.astype(jnp.bfloat16)


def with_ends(drawn, own_key, low, largest):
    extent = drawn.shape
    index_at = [jax.random.randint(jax.random.fold_in(own_key, axis), (), 0, extent[axis]) for axis in range(len(extent))]
    drawn = drawn.at[tuple(index_at)].set(low)
    longest = extent.index(max(extent))
    index_at[longest] = (index_at[longest] + 1) % extent[longest]
    return drawn.at[tuple(index_at)].set(largest)


def block_scale(key, shape, cuts, least, top_value):
    loudness, own = 1.0, jax.random.fold_in(key, 6)
    for axis_at, shards_of in cuts:
        steps = jnp.exp(jax.random.uniform(jax.random.fold_in(own, axis_at), (shards_of,), jnp.float32, least / len(cuts), top_value / len(cuts)))
        loudness = loudness * jnp.repeat(steps, shape[axis_at] // shards_of).reshape([-1 if axis == axis_at else 1 for axis in range(len(shape))])
    return loudness


def gaussian(key, dims, width, most, cuts=(), kind=jnp.bfloat16):
    result = jax.random.normal(key, dims, jnp.float32) * width
    if len(cuts) > 0:
        result = block_scale(key, dims, cuts, -0.22, 0.18) * result
    return jnp.clip(result, min=-most, max=most).astype(kind)


def setup_inputs(seed: int = 0) -> dict:
    streams_of = jax.random.split(jax.random.key(seed), 7)
    hidden = draw_hidden(jax.random.fold_in(streams_of[6], 71), 0)
    ref_hidden = draw_ref_hidden(jax.random.fold_in(streams_of[6], 71), 0)
    sampled = with_ends(jax.random.randint(streams_of[2], (TOKENS,), 0, V), jax.random.fold_in(streams_of[2], 1), 0, V - 1).astype(jnp.int32)
    advantage = gaussian(streams_of[3], (TOKENS,), 1.0, 4.0, ((0, 8),), jnp.float32)
    policy_head = draw_policy_head(jax.random.fold_in(streams_of[6], 71), 0)
    ref_head = draw_ref_head(jax.random.fold_in(streams_of[6], 71), 0)
    return {"hidden": hidden, "ref_hidden": ref_hidden, "sampled": sampled, "advantage": advantage, "policy_head": policy_head, "ref_head": ref_head}


def reference(hidden, ref_hidden, sampled, advantage, policy_head, ref_head):
    z = jnp.dot(hidden, policy_head, preferred_element_type=jnp.float32)
    r = jnp.dot(ref_hidden, ref_head, preferred_element_type=jnp.float32)
    lse_z = jax.nn.logsumexp(z, axis=1, keepdims=True)
    lse_r = jax.nn.logsumexp(r, axis=1, keepdims=True)
    lp = z - lse_z
    lq = r - lse_r
    probs = jnp.exp(lp)
    onehot = (jnp.arange(V, dtype=jnp.int32)[None, :] == sampled[:, None].astype(jnp.int32))
    logp = jnp.sum(jnp.where(onehot, lp, 0.0), axis=1)
    entropy = -jnp.sum(probs * lp, axis=1)
    kl = jnp.sum(probs * (lp - lq), axis=1)
    grad_logits = (-advantage[:, None] * (onehot.astype(jnp.float32) - probs)
                   + 0.1 * probs * (lp - lq - kl[:, None])
                   + 0.05 * probs * (lp + entropy[:, None])).astype(jnp.bfloat16)
    d_policy = jnp.dot(hidden.T, grad_logits, preferred_element_type=jnp.float32).astype(jnp.bfloat16)
    d_hidden = jnp.dot(grad_logits, policy_head.T, preferred_element_type=jnp.float32)
    return logp, entropy, kl, d_hidden, d_policy
```

```python
import functools

import jax
import jax.numpy as jnp
from jax import lax
from jax.experimental import pallas as pl
from jax.experimental.pallas import tpu as pltpu
from jax.sharding import Mesh, PartitionSpec as P

NX, NC, NZ, NY = 4, 2, 8, 4
OWN = 128
BF, F32, I32 = jnp.bfloat16, jnp.float32, jnp.int32
LIMIT = 24 * 1024 * 1024
VMEM, SMEM, HBM = pltpu.VMEM, pltpu.SMEM, pltpu.HBM


def params(**more):
    return pltpu.CompilerParams(vmem_limit_bytes=LIMIT, **more)


def in_hbm(a):
    return pltpu.with_memory_space_constraint(a, HBM)


def split(n, parts):
    step = -(-n // (16 * parts)) * 16
    return [(k, min(step, n - k)) for k in range(0, n, step)]


def cost(flops, nbytes, trans=0):
    return pl.CostEstimate(flops=int(flops), bytes_accessed=int(nbytes), transcendentals=int(trans))


def lanes(s):
    return pl.ds(pl.multiple_of(s * OWN, OWN), OWN)


def prep_kernel(piece, n_out, w_hbm, *refs):
    wt_hbm, wr_hbm = refs[0], refs[1 if n_out == 2 else 0]
    wbuf, tbuf, rbuf, in_sem, t_sem, r_sem = refs[n_out:]
    n, h, _ = wbuf.shape

    def load(s):
        return [
            pltpu.make_async_copy(w_hbm.at[pl.ds(k, m), lanes(s)], wbuf.at[s, pl.ds(k, m)], in_sem.at[s, i])
            for i, (k, m) in enumerate(split(h, 4))
        ]

    def store(s):
        copies = []
        for i, (k, m) in enumerate(split(OWN, 4)):
            rows = pl.ds(pl.multiple_of(s * OWN + k, 16), m)
            copies.append(pltpu.make_async_copy(tbuf.at[s, pl.ds(k, m)], wt_hbm.at[rows], t_sem.at[s, i]))
        if n_out == 2:
            for y in range(NY):
                copies.append(pltpu.make_async_copy(rbuf.at[s, y], wr_hbm.at[y, :, :, lanes(s)], r_sem.at[s, y]))
        return copies

    for s in range(n):
        for copy in load(s):
            copy.start()

    def step(s, _):
        for copy in load(s):
            copy.wait()
        w = wbuf[s]
        tbuf[s] = w.T
        if n_out == 2:
            fill = jnp.zeros((rbuf.shape[3] - piece, OWN), w.dtype)
            for z in range(NZ):
                for y in range(NY):
                    k = (z * NY + y) * piece
                    rbuf[s, y, z] = jnp.concatenate((w[k : k + piece], fill), axis=0)
        for copy in store(s):
            copy.start()
        return 0

    lax.fori_loop(0, n, step, 0)
    for s in range(n):
        for copy in store(s):
            copy.wait()


def prep(w, padded=None):
    h, width = w.shape
    n = width // OWN
    out_shape = [HBM((width, h), BF)]
    if padded:
        out_shape.append(HBM((NY, NZ, padded, width), BF))
    return pl.pallas_call(
        functools.partial(prep_kernel, h // (NZ * NY), len(out_shape)),
        out_shape=out_shape,
        in_specs=[pl.BlockSpec(memory_space=pl.ANY)],
        out_specs=[pl.BlockSpec(memory_space=pl.ANY)] * len(out_shape),
        scratch_shapes=[
            VMEM((n, h, OWN), BF),
            VMEM((n, OWN, h), BF),
            VMEM((n if padded else 1, NY, NZ, padded or 16, OWN), BF),
            pltpu.SemaphoreType.DMA((n, 4)),
            pltpu.SemaphoreType.DMA((n, 4)),
            pltpu.SemaphoreType.DMA((n, NY)),
        ],
        compiler_params=params(),
        cost_estimate=cost(0, 6 * h * width),
    )(in_hbm(w))


WT_PARTS = 8


def wt_loads(src, dst, sem):
    return [
        pltpu.make_async_copy(src.at[pl.ds(k, m)], dst.at[pl.ds(k, m)], sem.at[i])
        for i, (k, m) in enumerate(split(src.shape[0], WT_PARTS))
    ]


def head_kernel(plan, slots, n_in, n_prev, n_out, info_ref, wt_hbm, *refs):
    arrays = refs[:n_in]
    outs = refs[n_in + n_prev : n_in + n_prev + n_out]
    wt, xs, obuf, wt_sem, in_sem, out_sem, keep_sem = refs[n_in + n_prev + n_out :]
    wt_copies = wt_loads(wt_hbm, wt, wt_sem)
    for copy in wt_copies:
        copy.start()
    copies = []
    for i, (at, slot, rows) in enumerate(plan):
        first = pl.multiple_of(info_ref[slots + i], 16)
        src = arrays[at].at[pl.ds(0, rows)]
        copy = pltpu.make_async_copy(src, xs.at[pl.ds(first, rows), pl.ds(slot * OWN, OWN)], in_sem.at[i])
        copy.start()
        copies.append(copy)
    for copy in copies:
        copy.wait()
    done = []
    if n_out == 2:
        for s in range(slots):
            copy = pltpu.make_async_copy(xs.at[:, pl.ds(s * OWN, OWN)], outs[1].at[info_ref[s]], keep_sem.at[s])
            copy.start()
            done.append(copy)
    for copy in wt_copies:
        copy.wait()
    width = wt.shape[0]
    tile = width // 2

    def step(t, _):
        rows = pl.ds(pl.multiple_of(t * tile, tile), tile)
        acc = jnp.dot(wt[rows, :], xs[...], preferred_element_type=F32)
        for s in range(slots):
            obuf[s, rows, :] = acc[:, s * OWN : (s + 1) * OWN]
        return 0

    lax.fori_loop(0, width // tile, step, 0)
    for s in range(slots):
        copy = pltpu.make_async_copy(obuf.at[s], outs[0].at[info_ref[s]], out_sem.at[s])
        copy.start()
        done.append(copy)
    for copy in done:
        copy.wait()


def head_product(wt, pieces, slot_blocks, keep, prev=()):
    width, h = wt.shape
    slots = len(slot_blocks)
    arrays = [arr for arr, _, _, _ in pieces]
    plan = [(i, slot, rows) for i, (_, slot, _, rows) in enumerate(pieces)]
    info = jnp.stack([jnp.asarray(v, I32) for v in slot_blocks] + [jnp.asarray(f, I32) for _, _, f, _ in pieces])
    out_shape = [HBM((NX * NC, width, OWN), F32)]
    if keep:
        out_shape.append(HBM((NX * NC, h, OWN), BF))
    any_spec = pl.BlockSpec(memory_space=pl.ANY)
    n_in = len(arrays)
    return pl.pallas_call(
        functools.partial(head_kernel, plan, slots, n_in, len(prev), len(out_shape)),
        out_shape=out_shape,
        in_specs=[pl.BlockSpec(memory_space=SMEM)] + [any_spec] * (1 + n_in + len(prev)),
        out_specs=[any_spec] * len(out_shape),
        scratch_shapes=[
            VMEM((width, h), BF),
            VMEM((h, slots * OWN), BF),
            VMEM((slots, width, OWN), F32),
            pltpu.SemaphoreType.DMA((WT_PARTS,)),
            pltpu.SemaphoreType.DMA((len(plan),)),
            pltpu.SemaphoreType.DMA((slots,)),
            pltpu.SemaphoreType.DMA((slots,)),
        ],
        input_output_aliases={2 + n_in + k: k for k in range(len(prev))},
        compiler_params=params(),
        cost_estimate=cost(2 * width * h * slots * OWN, width * h * 2 + slots * OWN * (h * 2 + width * 4)),
    )(info, in_hbm(wt), *arrays, *prev)


def stats_rows(z, r, ids, first):
    col = (lax.broadcasted_iota(I32, z.shape, 0) + first).astype(F32)
    m_z = jnp.max(z, axis=0, keepdims=True)
    m_r = jnp.max(r, axis=0, keepdims=True)
    e = jnp.exp(z - m_z)
    rows = (
        m_z,
        jnp.sum(e, axis=0, keepdims=True),
        jnp.sum(e * z, axis=0, keepdims=True),
        jnp.sum(e * r, axis=0, keepdims=True),
        m_r,
        jnp.sum(jnp.exp(r - m_r), axis=0, keepdims=True),
        jnp.sum(jnp.where(col == ids, z, 0.0), axis=0, keepdims=True),
        jnp.zeros_like(m_z),
    )
    return jnp.concatenate(rows, axis=0)


def stats_kernel(n, info_ref, lab_ref, z_hbm, r_hbm, out_ref, zb, rb, sem):
    def load(k):
        at = info_ref[k + 1]
        return (
            pltpu.make_async_copy(z_hbm.at[at], zb.at[k], sem.at[0, k]),
            pltpu.make_async_copy(r_hbm.at[at], rb.at[k], sem.at[1, k]),
        )

    for k in range(n):
        for copy in load(k):
            copy.start()

    def step(k, _):
        for copy in load(k):
            copy.wait()
        at = info_ref[k + 1]
        out_ref[at] = stats_rows(zb[k], rb[k], lab_ref[at, 0:1], info_ref[0])
        return 0

    lax.fori_loop(0, n, step, 0)


def row_stats(first, blocks, z, r, labels):
    width, n = z.shape[1], len(blocks)
    info = jnp.stack([first] + [jnp.asarray(b, I32) for b in blocks])
    return pl.pallas_call(
        functools.partial(stats_kernel, n),
        out_shape=jax.ShapeDtypeStruct((z.shape[0], 8, OWN), F32),
        in_specs=[pl.BlockSpec(memory_space=SMEM), pl.BlockSpec(memory_space=VMEM)] + [pl.BlockSpec(memory_space=pl.ANY)] * 2,
        out_specs=pl.BlockSpec(memory_space=VMEM),
        scratch_shapes=[VMEM((n, width, OWN), F32), VMEM((n, width, OWN), F32), pltpu.SemaphoreType.DMA((2, n))],
        compiler_params=params(),
        cost_estimate=cost(12 * z.size, 6 * z.size, 2 * z.size),
    )(info, labels, in_hbm(z), in_hbm(r))


def late_kernel(plan, n_in, info_ref, lab_ref, wp_hbm, wr_hbm, *refs):
    arrays = refs[:n_in]
    z_out, r_out, x_out, st_out = refs[n_in + 4 : n_in + 8]
    wts, xs, obuf, stbuf, wt_sem, in_sem, out_sem, keep_sem, st_sem = refs[n_in + 8 :]
    wt_copies = [wt_loads(w, wts.at[k], wt_sem.at[k]) for k, w in enumerate((wp_hbm, wr_hbm))]
    copies = [[], []]
    for head in range(2):
        for copy in wt_copies[head]:
            copy.start()
        for i, (at, slot, rows) in enumerate(plan):
            first = pl.multiple_of(info_ref[3 + i], 16)
            dst = xs.at[head, pl.ds(first, rows), pl.ds(slot * OWN, OWN)]
            copy = pltpu.make_async_copy(arrays[at].at[pl.ds(head * rows, rows)], dst, in_sem.at[head, i])
            copy.start()
            copies[head].append(copy)
    width = wts.shape[1]
    tile = width // 2
    done = []
    for head, out in enumerate((z_out, r_out)):
        for copy in copies[head]:
            copy.wait()
        for copy in wt_copies[head]:
            copy.wait()

        def step(t, _):
            rows = pl.ds(pl.multiple_of(t * tile, tile), tile)
            acc = jnp.dot(wts[head, rows, :], xs[head], preferred_element_type=F32)
            for s in range(2):
                obuf[head, s, rows, :] = acc[:, s * OWN : (s + 1) * OWN]
            return 0

        lax.fori_loop(0, width // tile, step, 0)
        for s in range(2):
            copy = pltpu.make_async_copy(obuf.at[head, s], out.at[info_ref[1 + s]], out_sem.at[head, s])
            copy.start()
            done.append(copy)
            if head == 0:
                copy = pltpu.make_async_copy(xs.at[0, :, pl.ds(s * OWN, OWN)], x_out.at[info_ref[1 + s]], keep_sem.at[s])
                copy.start()
                done.append(copy)
    for s in range(2):
        stbuf[s] = stats_rows(obuf[0, s], obuf[1, s], lab_ref[info_ref[1 + s], 0:1], info_ref[0])
        copy = pltpu.make_async_copy(stbuf.at[s], st_out.at[info_ref[1 + s]], st_sem.at[s])
        copy.start()
        done.append(copy)
    for copy in done:
        copy.wait()


def late_product(first, labels, wt_p, wt_r, pieces, blocks, z, r, x_all, stats):
    width, h = wt_p.shape
    plan = [(i, slot, rows) for i, (_, slot, _, rows) in enumerate(pieces)]
    info = jnp.stack([first] + [jnp.asarray(v, I32) for v in blocks] + [jnp.asarray(f, I32) for _, _, f, _ in pieces])
    n_in = len(pieces)
    hbm = pl.BlockSpec(memory_space=pl.ANY)
    prev = [in_hbm(a) for a in (z, r, x_all, stats)]
    return pl.pallas_call(
        functools.partial(late_kernel, plan, n_in),
        out_shape=[HBM(a.shape, a.dtype) for a in prev],
        in_specs=[pl.BlockSpec(memory_space=SMEM), pl.BlockSpec(memory_space=VMEM)] + [hbm] * (2 + n_in + 4),
        out_specs=[hbm] * 4,
        scratch_shapes=[
            VMEM((2, width, h), BF),
            VMEM((2, h, 2 * OWN), BF),
            VMEM((2, 2, width, OWN), F32),
            VMEM((2, 8, OWN), F32),
            pltpu.SemaphoreType.DMA((2, WT_PARTS)),
            pltpu.SemaphoreType.DMA((2, n_in)),
            pltpu.SemaphoreType.DMA((2, 2)),
            pltpu.SemaphoreType.DMA((2,)),
            pltpu.SemaphoreType.DMA((2,)),
        ],
        input_output_aliases={4 + n_in + k: k for k in range(4)},
        compiler_params=params(),
        cost_estimate=cost(8 * width * h * OWN, 4 * width * h + 8 * OWN * (h + width)),
    )(info, labels, in_hbm(wt_p), in_hbm(wt_r), *[arr for arr, _, _, _ in pieces], *prev)


def merge_kernel(in_ref, out_ref):
    row = lambda k: in_ref[:, :, k : k + 1]
    for top, sums in ((0, (1, 2, 3)), (4, (5,))):
        peak = jnp.max(row(top), axis=0)
        scale = jnp.exp(row(top) - peak[None])
        out_ref[:, top : top + 1] = peak
        for k in sums:
            out_ref[:, k : k + 1] = jnp.sum(scale * row(k), axis=0)
    for k in (6, 7):
        out_ref[:, k : k + 1] = jnp.sum(row(k), axis=0)


def merge(stats):
    return pl.pallas_call(
        merge_kernel,
        out_shape=jax.ShapeDtypeStruct(stats.shape[1:], F32),
        compiler_params=params(),
        cost_estimate=cost(10 * stats.size, 5 * stats.size),
    )(stats)


def by_xor(n, k):
    return [(i, i ^ k) for i in range(n)]


def by_shift(n, k):
    return [(i, (i + k) % n) for i in range(n)]


def all_merge(stats):
    stats = merge(jnp.stack((stats, lax.ppermute(stats, "core", by_xor(NC, 1)))))
    for axes, n in ((("x", "y"), NX * NY), ("z", NZ)):
        copies = jnp.broadcast_to(stats[None], (n, *stats.shape))
        stats = merge(lax.all_to_all(copies, axes, split_axis=0, concat_axis=0, tiled=True))
    return stats


def row_results(st):
    lse_z = st[0:1] + jnp.log(st[1:2])
    lse_r = st[4:5] + jnp.log(st[5:6])
    entropy = lse_z - st[2:3] / st[1:2]
    kl = (st[2:3] - st[3:4]) / st[1:2] - lse_z + lse_r
    return lse_z, lse_r, entropy, kl


def grad_of(z, r, ids, adv, st, first):
    col = (lax.broadcasted_iota(I32, z.shape, 0) + first).astype(F32)
    lse_z, lse_r, entropy, kl = row_results(st)
    lp = z - lse_z
    lq = r - lse_r
    p = jnp.exp(lp)
    hot = jnp.where(col == ids, 1.0, 0.0)
    return (-adv * (hot - p) + 0.1 * p * (lp - lq - kl) + 0.05 * p * (lp + entropy)).astype(BF)


W_PARTS = 2


def w_loads(y, w_hbm, wb, sem):
    return [
        pltpu.make_async_copy(w_hbm.at[y, pl.ds(k, m)], wb.at[y, pl.ds(k, m)], sem.at[y, i])
        for i, (k, m) in enumerate(split(wb.shape[1], W_PARTS))
    ]


def term_loop(info_ref, base, load_w, wb, rows_of, far_ref, near_ref):
    def step(y, _):
        for copy in load_w(y):
            copy.wait()
        rows = jnp.concatenate([rows_of(x) for x in range(NX)], axis=1)
        acc = jnp.dot(wb[y], rows, preferred_element_type=F32).astype(BF)
        for x in range(NX):
            at = base + 2 * (y * NX + x)
            group, k = info_ref[at], info_ref[at + 1]

            @pl.when(group == 0)
            def _():
                far_ref[k] = acc[:, x * OWN : (x + 1) * OWN]

            @pl.when(group > 0)
            def _():
                near_ref[group - 1, k] = acc[:, x * OWN : (x + 1) * OWN]

        return 0

    lax.fori_loop(0, NY, step, 0)


def grad_term_kernel(info_ref, lab_ref, st_ref, z_hbm, r_hbm, w_hbm, g_hbm, far_ref, near_ref, zb, rb, wb, gb, in_sem, w_sem, g_sem):
    n = zb.shape[0]

    def load(k):
        return (
            pltpu.make_async_copy(z_hbm.at[k], zb.at[k], in_sem.at[0, k]),
            pltpu.make_async_copy(r_hbm.at[k], rb.at[k], in_sem.at[1, k]),
        )

    def load_w(y):
        return w_loads(y, w_hbm, wb, w_sem)

    def store(k):
        return pltpu.make_async_copy(gb.at[k], g_hbm.at[k], g_sem.at[k])

    for k in range(n):
        for copy in load(k):
            copy.start()
    for y in range(NY):
        for copy in load_w(y):
            copy.start()

    def step(k, _):
        for copy in load(k):
            copy.wait()
        gb[k] = grad_of(zb[k], rb[k], lab_ref[k, 0:1], lab_ref[k, 1:2], st_ref[k], info_ref[0])
        store(k).start()
        return 0

    lax.fori_loop(0, n, step, 0)
    term_loop(info_ref, 2, load_w, wb, lambda x: gb[info_ref[1] * NX + x], far_ref, near_ref)
    for k in range(n):
        store(k).wait()


def own_term_kernel(info_ref, w_hbm, g_hbm, far_ref, near_ref, wb, gb, w_sem, g_sem):
    def load_w(y):
        return w_loads(y, w_hbm, wb, w_sem)

    def load_g(x):
        return pltpu.make_async_copy(g_hbm.at[info_ref[0] * NX + x], gb.at[x], g_sem.at[x])

    for x in range(NX):
        load_g(x).start()
    for y in range(NY):
        for copy in load_w(y):
            copy.start()
    for x in range(NX):
        load_g(x).wait()
    term_loop(info_ref, 1, load_w, wb, lambda x: gb[x], far_ref, near_ref)


def term_places(to_x, ix, iy):
    out = []
    for y in range(NY):
        for x in range(NX):
            distance = jnp.where(to_x, x - ix, y - iy) % NX
            group = jnp.where(distance == 0, 3, jnp.where(distance == 1, 1, jnp.where(distance == 2, 0, 2)))
            out += [group, jnp.where(to_x, y, x)]
    return out


def pack(values):
    return jnp.stack([jnp.asarray(v, I32) for v in values])


def term_shapes(m):
    return [jax.ShapeDtypeStruct((NX, m, OWN), BF), jax.ShapeDtypeStruct((NX - 1, NX, m, OWN), BF)]


def grad_and_terms(first, core, places, labels, stats, z, r, w):
    n, width, _ = z.shape
    m = w.shape[1]
    hbm, vmem = pl.BlockSpec(memory_space=pl.ANY), pl.BlockSpec(memory_space=VMEM)
    return pl.pallas_call(
        grad_term_kernel,
        out_shape=[HBM(z.shape, BF)] + term_shapes(m),
        in_specs=[pl.BlockSpec(memory_space=SMEM), vmem, vmem, hbm, hbm, hbm],
        out_specs=[hbm, vmem, vmem],
        scratch_shapes=[
            VMEM(z.shape, F32),
            VMEM(z.shape, F32),
            VMEM(w.shape, BF),
            VMEM(z.shape, BF),
            pltpu.SemaphoreType.DMA((2, n)),
            pltpu.SemaphoreType.DMA((NY, W_PARTS)),
            pltpu.SemaphoreType.DMA((n,)),
        ],
        compiler_params=params(),
        cost_estimate=cost(2 * w.size * NX * OWN + 16 * z.size, 10 * z.size + 2 * w.size + 8 * m * NX * OWN, z.size),
    )(pack([first, core] + places), labels, stats, in_hbm(z), in_hbm(r), in_hbm(w))


def own_terms(core, places, g, w):
    m, width = w.shape[1:]
    hbm, vmem = pl.BlockSpec(memory_space=pl.ANY), pl.BlockSpec(memory_space=VMEM)
    return pl.pallas_call(
        own_term_kernel,
        out_shape=term_shapes(m),
        in_specs=[pl.BlockSpec(memory_space=SMEM), hbm, hbm],
        out_specs=[vmem, vmem],
        scratch_shapes=[
            VMEM(w.shape, BF),
            VMEM((NX, width, OWN), BF),
            pltpu.SemaphoreType.DMA((NY, W_PARTS)),
            pltpu.SemaphoreType.DMA((NX,)),
        ],
        compiler_params=params(),
        cost_estimate=cost(2 * w.size * NX * OWN, 2 * w.size + g.size + 8 * m * NX * OWN),
    )(pack([core] + places), in_hbm(w), in_hbm(g))


def d_policy_kernel(x_hbm, g_hbm, out_hbm, xb, gb, ob, x_sem, g_sem, o_sem):
    tiles, _, m, _ = xb.shape

    def rows(t):
        return pl.ds(pl.multiple_of(t * m, 16), m)

    n = gb.shape[0]

    def load(t):
        return pltpu.make_async_copy(x_hbm.at[:, rows(t)], xb.at[t], x_sem.at[t])

    def store(t):
        return pltpu.make_async_copy(ob.at[t], out_hbm.at[rows(t)], o_sem.at[t])

    load_g = [pltpu.make_async_copy(g_hbm.at[b], gb.at[b], g_sem.at[b]) for b in range(n)]
    for copy in load_g:
        copy.start()
    for t in range(tiles):
        load(t).start()
    for copy in load_g:
        copy.wait()

    def step(t, _):
        load(t).wait()
        acc = 0.0
        for j in range(0, NX * NC, 2):
            lhs = jnp.concatenate((xb[t, j], xb[t, j + 1]), axis=1)
            rhs = jnp.concatenate((gb[j], gb[j + 1]), axis=1)
            acc = acc + lax.dot_general(lhs, rhs, (((1,), (1,)), ((), ())), preferred_element_type=F32)
        ob[t] = acc.astype(BF)
        store(t).start()
        return 0

    lax.fori_loop(0, tiles, step, 0)
    for t in range(tiles):
        store(t).wait()


def d_policy_of(x, g):
    n, h, _ = x.shape
    width = g.shape[1]
    tiles = 6
    m = h // tiles
    hbm = pl.BlockSpec(memory_space=pl.ANY)
    return pl.pallas_call(
        d_policy_kernel,
        out_shape=jax.ShapeDtypeStruct((h, width), BF),
        in_specs=[hbm, hbm],
        out_specs=hbm,
        scratch_shapes=[
            VMEM((tiles, n, m, OWN), BF),
            VMEM(g.shape, BF),
            VMEM((tiles, m, width), BF),
            pltpu.SemaphoreType.DMA((tiles,)),
            pltpu.SemaphoreType.DMA((n,)),
            pltpu.SemaphoreType.DMA((tiles,)),
        ],
        compiler_params=params(),
        cost_estimate=cost(2 * h * width * n * OWN, 2 * (x.size + g.size + h * width)),
    )(in_hbm(x), in_hbm(g))


UP_X, DOWN_X = by_shift(NX, 1), by_shift(NX, NX - 1)
UP_Y, DOWN_Y = by_shift(NY, 1), by_shift(NY, NY - 1)
ALL = ("x", "core", "z", "y")


def swap(a):
    return lax.ppermute(a, "core", by_xor(NC, 1))


def cut(a, first, n):
    return lax.dynamic_slice_in_dim(a, first, n, 0)


def core_route(d, second):
    pairs = []
    for x in range(NX):
        for c in range(NC):
            for z in range(NZ):
                for y in range(NY):
                    along_x = (c == 0) != second
                    x2, y2 = ((x + d) % NX, y) if along_x else (x, (y + d) % NY)
                    pairs.append((((x * NC + c) * NZ + z) * NY + y, ((x2 * NC + c) * NZ + z) * NY + y2))
    return pairs


def label_rows(ids, adv):
    top = lax.reduce_precision(adv, 8, 7)
    middle = lax.reduce_precision(adv - top, 8, 7)
    parts = [(ids >> 12).astype(F32), ((ids >> 6) & 63).astype(F32), (ids & 63).astype(F32), top, middle, adv - top - middle]
    return jnp.pad(jnp.stack(parts).astype(BF), ((0, 10), (0, 0)))


def add(a, b):
    return (a.astype(F32) + b.astype(F32)).astype(BF)


def after(value, *first):
    return lax.optimization_barrier((value, *first))[0]


def shards(hidden, ref_hidden, sampled, advantage, policy_head, ref_head):
    ix, ic, iz, iy = (lax.axis_index(a) for a in ALL)
    h, width = policy_head.shape
    half, quarter = h // 2, h // 4
    odd = iy % 2
    lo, hi, skip = odd * half, (1 - odd) * half, odd * quarter
    piece = h // (NZ * NY)
    padded = -(-piece // 16) * 16

    def block(d, other):
        return (ic ^ other) * NX + (ix + d) % NX

    own_p, own_r = hidden.T, ref_hidden.T
    marks = label_rows(sampled, advantage)
    a_p = lax.ppermute(jnp.concatenate((cut(own_p, lo, half), marks), axis=0), "x", DOWN_X)
    b_p = lax.ppermute(jnp.concatenate((cut(own_p, hi, half), marks), axis=0), "x", UP_X)
    a_r = lax.ppermute(cut(own_r, lo, half), "x", DOWN_X)
    b_r = lax.ppermute(cut(own_r, hi, half), "x", UP_X)

    wt_p, w_yz = prep(policy_head, padded)
    w_yz = w_yz.reshape(NY, NZ * padded, width)
    a_p, b_p, wt_p = lax.optimization_barrier((a_p, b_p, wt_p))
    a2_p = lax.ppermute(a_p, "y", UP_Y)
    b2_p = lax.ppermute(b_p, "y", DOWN_Y)
    there = [swap(arr) for arr in (own_p, a_p, b_p)]
    a_r, b_r, a2_p, b2_p, *there = lax.optimization_barrier((a_r, b_r, a2_p, b2_p, *there))
    c = lax.ppermute(jnp.concatenate((cut(a_p, skip, quarter), cut(a_r, skip, quarter), a_p[half:]), axis=0), "x", DOWN_X)
    d = lax.ppermute(jnp.concatenate((cut(b_p, skip, quarter), cut(b_r, skip, quarter), b_p[half:]), axis=0), "x", UP_X)
    a2_r = lax.ppermute(a_r, "y", UP_Y)
    b2_r = lax.ppermute(b_r, "y", DOWN_Y)
    rest = quarter - skip
    there += [swap(a2_p), swap(b2_p)]

    def early(here, there):
        out = []
        for k, (slot, f, rows) in enumerate(((0, 0, h), (2, lo, half), (4, hi, half), (2, hi, half), (4, lo, half))):
            out += [(here[k], slot, f, rows), (there[k], slot + 1, f, rows)]
        return out

    blocks = [block(dist, s) for dist in (0, 1, 3) for s in (0, 1)]
    z, x_all = head_product(wt_p, early((own_p, a_p, b_p, a2_p, b2_p), there), blocks, keep=True)
    c, d, z = lax.optimization_barrier((c, d, z))
    (wt_r,) = prep(after(ref_head, z))
    c2 = lax.ppermute(c, "y", UP_Y)
    d2 = lax.ppermute(d, "y", DOWN_Y)
    here_r = (own_r, a_r, b_r, a2_r, b2_r)
    there_r = [swap(after(arr, z)) for arr in here_r]
    (r,) = head_product(wt_r, early(here_r, there_r), blocks, keep=False)
    c2, d2, r = lax.optimization_barrier((c2, d2, r))

    last = (c, d, c2, d2)
    last_there = [swap(arr) for arr in last]
    marks = jnp.stack((marks, a_p[half:], c[2 * quarter :], b_p[half:]))
    marks = jnp.stack((marks, jnp.stack((swap(marks[0]), there[1][half:], last_there[0][2 * quarter :], there[2][half:]))))
    marks = marks[:, :, :6].astype(F32)
    labels = jnp.stack((marks[:, :, 0] * 4096.0 + marks[:, :, 1] * 64.0 + marks[:, :, 2], marks[:, :, 3] + marks[:, :, 4] + marks[:, :, 5]), axis=2)
    labels = jnp.where(ic == 0, labels, labels[::-1])
    labels = jnp.concatenate((labels, labels), axis=1)
    labels = lax.dynamic_slice_in_dim(labels, NX - ix, NX, 1).reshape(NC * NX, 2, OWN)

    first = ((((ix * NC + ic) * NZ + iz) * NY + iy) * width).astype(I32)
    stats = row_stats(first, blocks, z, r, labels)
    late = []
    for arr, arr_there, f in zip(last, last_there, (lo + skip, hi + skip, hi + rest, lo + rest)):
        late += [(arr, 0, f, quarter), (arr_there, 1, f, quarter)]
    z, r, x_all, stats = late_product(first, labels, wt_p, wt_r, late, [block(2, s) for s in (0, 1)], z, r, x_all, stats)

    stats = all_merge(stats)
    g, far_other, near_other = grad_and_terms(first, 1 - ic, term_places(ic == 1, ix, iy), labels, stats, z, r, w_yz)
    far_mine, near_mine = own_terms(ic, term_places(ic == 0, ix, iy), g, w_yz)
    far_other = swap(far_other)
    near_other = swap(near_other)
    far = add(far_mine, far_other)
    via_up = lax.ppermute(far[:2], ALL, core_route(1, False))
    via_down = lax.ppermute(far[2:], ALL, core_route(-1, False))
    near = near_mine.astype(F32) + near_other.astype(F32)
    to_up = jnp.concatenate(((near[0, :2] + via_up.astype(F32)).astype(BF), near[0, 2:].astype(BF)), axis=0)
    to_down = jnp.concatenate((near[1, :2].astype(BF), (near[1, 2:] + via_down.astype(F32)).astype(BF)), axis=0)
    from_down = lax.ppermute(to_up, ALL, core_route(1, False))
    from_up = lax.ppermute(to_down, ALL, core_route(-1, False))
    d_policy = d_policy_of(x_all, after(g, to_up, to_down))
    from_down, from_up, d_policy = lax.optimization_barrier((from_down, from_up, d_policy))
    parts = near[2] + from_down.astype(F32) + from_up.astype(F32)

    at = jnp.where(ic == 0, iy, ix)
    total = lax.dynamic_index_in_dim(parts, at, 0, keepdims=False)
    parts = parts.astype(BF)
    for dist in (1, 3, 2):
        part = lax.dynamic_index_in_dim(parts, (at + dist) % NX, 0, keepdims=False)
        total = total + lax.ppermute(part, ALL, core_route(dist, True)).astype(F32)
    total = total.astype(BF).reshape(NZ, padded, OWN)
    got = lax.all_to_all(total, "z", split_axis=0, concat_axis=0, tiled=True)
    d_hidden = jnp.sum(got.astype(F32), axis=0)[:piece].T

    mine = lax.dynamic_index_in_dim(stats, block(0, 0), 0, keepdims=False)
    lse_z, _, entropy, kl = row_results(mine)
    return (mine[6] - lse_z[0], entropy[0], kl[0], d_hidden, d_policy)


def solution(mesh):
    fine = Mesh(mesh.devices.reshape(NX, NC, NZ, NY), ("x", "core", "z", "y"))
    dp, vocab = ("x", "core"), ("z", "y")
    everybody = dp + vocab
    in_specs = (P(dp, None), P(dp, None), P(dp), P(dp), P(None, everybody), P(None, everybody))
    out_specs = (P(dp), P(dp), P(dp), P(dp, vocab), P(None, everybody))
    return jax.shard_map(shards, mesh=fine, in_specs=in_specs, out_specs=out_specs, check_vma=False)
```

```python
import functools

import jax
import jax.numpy as jnp
from jax import lax
from jax.experimental import pallas as pl
from jax.experimental.pallas import tpu as pltpu
from jax.sharding import Mesh, PartitionSpec as P

NX, NC, NZ, NY = 4, 2, 8, 4
OWN = 128
BF, F32, I32 = jnp.bfloat16, jnp.float32, jnp.int32
LIMIT, SMALL = 24 * 1024 * 1024, 16 * 1024 * 1024
VMEM, SMEM, HBM = pltpu.VMEM, pltpu.SMEM, pltpu.HBM


def params(limit=LIMIT):
    return pltpu.CompilerParams(vmem_limit_bytes=limit)


def in_hbm(a):
    return pltpu.with_memory_space_constraint(a, HBM)


def split(n, parts):
    step = -(-n // (16 * parts)) * 16
    return [(k, min(step, n - k)) for k in range(0, n, step)]


def cost(flops, nbytes, trans=0):
    return pl.CostEstimate(flops=int(flops), bytes_accessed=int(nbytes), transcendentals=int(trans))


def lanes(s):
    return pl.ds(pl.multiple_of(s * OWN, OWN), OWN)


def prep_kernel(piece, n_out, w_hbm, *refs):
    wt_hbm, wr_hbm = refs[0], refs[1 if n_out == 2 else 0]
    wbuf, tbuf, rbuf, in_sem, t_sem, r_sem = refs[n_out:]
    n, h, _ = wbuf.shape

    def load(s):
        return [
            pltpu.make_async_copy(w_hbm.at[pl.ds(k, m), lanes(s)], wbuf.at[s, pl.ds(k, m)], in_sem.at[s, i])
            for i, (k, m) in enumerate(split(h, 4))
        ]

    def store(s):
        copies = []
        for i, (k, m) in enumerate(split(OWN, 4)):
            rows = pl.ds(pl.multiple_of(s * OWN + k, 16), m)
            copies.append(pltpu.make_async_copy(tbuf.at[s, pl.ds(k, m)], wt_hbm.at[rows], t_sem.at[s, i]))
        if n_out == 2:
            for y in range(NY):
                copies.append(pltpu.make_async_copy(rbuf.at[s, y], wr_hbm.at[y, :, :, lanes(s)], r_sem.at[s, y]))
        return copies

    for s in range(n):
        for copy in load(s):
            copy.start()

    def step(s, _):
        for copy in load(s):
            copy.wait()
        w = wbuf[s]
        tbuf[s] = w.T
        if n_out == 2:
            fill = jnp.zeros((rbuf.shape[3] - piece, OWN), w.dtype)
            for z in range(NZ):
                for y in range(NY):
                    k = (z * NY + y) * piece
                    rbuf[s, y, z] = jnp.concatenate((w[k : k + piece], fill), axis=0)
        for copy in store(s):
            copy.start()
        return 0

    lax.fori_loop(0, n, step, 0)
    for s in range(n):
        for copy in store(s):
            copy.wait()


def prep(w, padded=None):
    h, width = w.shape
    n = width // OWN
    out_shape = [HBM((width, h), BF)]
    if padded:
        out_shape.append(HBM((NY, NZ, padded, width), BF))
    return pl.pallas_call(
        functools.partial(prep_kernel, h // (NZ * NY), len(out_shape)),
        out_shape=out_shape,
        in_specs=[pl.BlockSpec(memory_space=pl.ANY)],
        out_specs=[pl.BlockSpec(memory_space=pl.ANY)] * len(out_shape),
        scratch_shapes=[
            VMEM((n, h, OWN), BF),
            VMEM((n, OWN, h), BF),
            VMEM((n if padded else 1, NY, NZ, padded or 16, OWN), BF),
            pltpu.SemaphoreType.DMA((n, 4)),
            pltpu.SemaphoreType.DMA((n, 4)),
            pltpu.SemaphoreType.DMA((n, NY)),
        ],
        compiler_params=params(SMALL),
        cost_estimate=cost(0, 6 * h * width),
    )(in_hbm(w))


WT_PARTS = 8


def wt_loads(src, dst, sem):
    return [
        pltpu.make_async_copy(src.at[pl.ds(k, m)], dst.at[pl.ds(k, m)], sem.at[i])
        for i, (k, m) in enumerate(split(src.shape[0], WT_PARTS))
    ]


def head_kernel(plan, slots, n_in, n_prev, n_out, info_ref, wt_hbm, *refs):
    arrays = refs[:n_in]
    outs = refs[n_in + n_prev : n_in + n_prev + n_out]
    wt, xs, obuf, wt_sem, in_sem, out_sem, keep_sem = refs[n_in + n_prev + n_out :]
    wt_copies = wt_loads(wt_hbm, wt, wt_sem)
    for copy in wt_copies:
        copy.start()
    copies = []
    for i, (at, slot, rows) in enumerate(plan):
        first = pl.multiple_of(info_ref[slots + i], 16)
        src = arrays[at].at[pl.ds(0, rows)]
        copy = pltpu.make_async_copy(src, xs.at[pl.ds(first, rows), pl.ds(slot * OWN, OWN)], in_sem.at[i])
        copy.start()
        copies.append(copy)
    for copy in copies:
        copy.wait()
    done = []
    if n_out == 2:
        for s in range(slots):
            copy = pltpu.make_async_copy(xs.at[:, pl.ds(s * OWN, OWN)], outs[1].at[info_ref[s]], keep_sem.at[s])
            copy.start()
            done.append(copy)
    for copy in wt_copies:
        copy.wait()
    width = wt.shape[0]
    tile = width // 2

    def step(t, _):
        rows = pl.ds(pl.multiple_of(t * tile, tile), tile)
        acc = jnp.dot(wt[rows, :], xs[...], preferred_element_type=F32)
        for s in range(slots):
            obuf[s, rows, :] = acc[:, s * OWN : (s + 1) * OWN]
        return 0

    lax.fori_loop(0, width // tile, step, 0)
    for s in range(slots):
        copy = pltpu.make_async_copy(obuf.at[s], outs[0].at[info_ref[s]], out_sem.at[s])
        copy.start()
        done.append(copy)
    for copy in done:
        copy.wait()


def head_product(wt, pieces, slot_blocks, keep, prev=()):
    width, h = wt.shape
    slots = len(slot_blocks)
    arrays = [arr for arr, _, _, _ in pieces]
    plan = [(i, slot, rows) for i, (_, slot, _, rows) in enumerate(pieces)]
    info = jnp.stack([jnp.asarray(v, I32) for v in slot_blocks] + [jnp.asarray(f, I32) for _, _, f, _ in pieces])
    out_shape = [HBM((NX * NC, width, OWN), F32)]
    if keep:
        out_shape.append(HBM((NX * NC, h, OWN), BF))
    any_spec = pl.BlockSpec(memory_space=pl.ANY)
    n_in = len(arrays)
    return pl.pallas_call(
        functools.partial(head_kernel, plan, slots, n_in, len(prev), len(out_shape)),
        out_shape=out_shape,
        in_specs=[pl.BlockSpec(memory_space=SMEM)] + [any_spec] * (1 + n_in + len(prev)),
        out_specs=[any_spec] * len(out_shape),
        scratch_shapes=[
            VMEM((width, h), BF),
            VMEM((h, slots * OWN), BF),
            VMEM((slots, width, OWN), F32),
            pltpu.SemaphoreType.DMA((WT_PARTS,)),
            pltpu.SemaphoreType.DMA((len(plan),)),
            pltpu.SemaphoreType.DMA((slots,)),
            pltpu.SemaphoreType.DMA((slots,)),
        ],
        input_output_aliases={2 + n_in + k: k for k in range(len(prev))},
        compiler_params=params(SMALL),
        cost_estimate=cost(2 * width * h * slots * OWN, width * h * 2 + slots * OWN * (h * 2 + width * 4)),
    )(info, in_hbm(wt), *arrays, *prev)


def stats_rows(z, r, ids, first):
    col = (lax.broadcasted_iota(I32, z.shape, 0) + first).astype(F32)
    m_z = jnp.max(z, axis=0, keepdims=True)
    m_r = jnp.max(r, axis=0, keepdims=True)
    e = jnp.exp(z - m_z)
    rows = (
        m_z,
        jnp.sum(e, axis=0, keepdims=True),
        jnp.sum(e * z, axis=0, keepdims=True),
        jnp.sum(e * r, axis=0, keepdims=True),
        m_r,
        jnp.sum(jnp.exp(r - m_r), axis=0, keepdims=True),
        jnp.sum(jnp.where(col == ids, z, 0.0), axis=0, keepdims=True),
        jnp.zeros_like(m_z),
    )
    return jnp.concatenate(rows, axis=0)


def stats_kernel(n, info_ref, lab_ref, z_hbm, r_hbm, out_ref, zb, rb, sem):
    def load(k):
        at = info_ref[k + 1]
        return (
            pltpu.make_async_copy(z_hbm.at[at], zb.at[k], sem.at[0, k]),
            pltpu.make_async_copy(r_hbm.at[at], rb.at[k], sem.at[1, k]),
        )

    for k in range(n):
        for copy in load(k):
            copy.start()

    def step(k, _):
        for copy in load(k):
            copy.wait()
        at = info_ref[k + 1]
        out_ref[at] = stats_rows(zb[k], rb[k], lab_ref[at, 0:1], info_ref[0])
        return 0

    lax.fori_loop(0, n, step, 0)


def row_stats(first, blocks, z, r, labels):
    width, n = z.shape[1], len(blocks)
    info = jnp.stack([first] + [jnp.asarray(b, I32) for b in blocks])
    return pl.pallas_call(
        functools.partial(stats_kernel, n),
        out_shape=jax.ShapeDtypeStruct((z.shape[0], 8, OWN), F32),
        in_specs=[pl.BlockSpec(memory_space=SMEM), pl.BlockSpec(memory_space=VMEM)] + [pl.BlockSpec(memory_space=pl.ANY)] * 2,
        out_specs=pl.BlockSpec(memory_space=VMEM),
        scratch_shapes=[VMEM((n, width, OWN), F32), VMEM((n, width, OWN), F32), pltpu.SemaphoreType.DMA((2, n))],
        compiler_params=params(SMALL),
        cost_estimate=cost(12 * z.size, 6 * z.size, 2 * z.size),
    )(info, labels, in_hbm(z), in_hbm(r))


def late_kernel(plan, n_in, info_ref, lab_ref, wp_hbm, wr_hbm, *refs):
    arrays = refs[:n_in]
    z_out, r_out, x_out, st_out = refs[n_in + 4 : n_in + 8]
    wts, xs, obuf, stbuf, wt_sem, in_sem, out_sem, keep_sem, st_sem = refs[n_in + 8 :]
    wt_copies = [wt_loads(w, wts.at[k], wt_sem.at[k]) for k, w in enumerate((wp_hbm, wr_hbm))]
    copies = [[], []]
    for head in range(2):
        for copy in wt_copies[head]:
            copy.start()
        for i, (at, slot, rows) in enumerate(plan):
            first = pl.multiple_of(info_ref[3 + i], 16)
            dst = xs.at[head, pl.ds(first, rows), pl.ds(slot * OWN, OWN)]
            copy = pltpu.make_async_copy(arrays[at].at[pl.ds(head * rows, rows)], dst, in_sem.at[head, i])
            copy.start()
            copies[head].append(copy)
    width = wts.shape[1]
    tile = width // 2
    done = []
    for head, out in enumerate((z_out, r_out)):
        for copy in copies[head]:
            copy.wait()
        for copy in wt_copies[head]:
            copy.wait()

        def step(t, _):
            rows = pl.ds(pl.multiple_of(t * tile, tile), tile)
            acc = jnp.dot(wts[head, rows, :], xs[head], preferred_element_type=F32)
            for s in range(2):
                obuf[head, s, rows, :] = acc[:, s * OWN : (s + 1) * OWN]
            return 0

        lax.fori_loop(0, width // tile, step, 0)
        for s in range(2):
            copy = pltpu.make_async_copy(obuf.at[head, s], out.at[info_ref[1 + s]], out_sem.at[head, s])
            copy.start()
            done.append(copy)
            if head == 0:
                copy = pltpu.make_async_copy(xs.at[0, :, pl.ds(s * OWN, OWN)], x_out.at[info_ref[1 + s]], keep_sem.at[s])
                copy.start()
                done.append(copy)
    for s in range(2):
        stbuf[s] = stats_rows(obuf[0, s], obuf[1, s], lab_ref[info_ref[1 + s], 0:1], info_ref[0])
        copy = pltpu.make_async_copy(stbuf.at[s], st_out.at[info_ref[1 + s]], st_sem.at[s])
        copy.start()
        done.append(copy)
    for copy in done:
        copy.wait()


def late_product(first, labels, wt_p, wt_r, pieces, blocks, z, r, x_all, stats):
    width, h = wt_p.shape
    plan = [(i, slot, rows) for i, (_, slot, _, rows) in enumerate(pieces)]
    info = jnp.stack([first] + [jnp.asarray(v, I32) for v in blocks] + [jnp.asarray(f, I32) for _, _, f, _ in pieces])
    n_in = len(pieces)
    hbm = pl.BlockSpec(memory_space=pl.ANY)
    prev = [in_hbm(a) for a in (z, r, x_all, stats)]
    return pl.pallas_call(
        functools.partial(late_kernel, plan, n_in),
        out_shape=[HBM(a.shape, a.dtype) for a in prev],
        in_specs=[pl.BlockSpec(memory_space=SMEM), pl.BlockSpec(memory_space=VMEM)] + [hbm] * (2 + n_in + 4),
        out_specs=[hbm] * 4,
        scratch_shapes=[
            VMEM((2, width, h), BF),
            VMEM((2, h, 2 * OWN), BF),
            VMEM((2, 2, width, OWN), F32),
            VMEM((2, 8, OWN), F32),
            pltpu.SemaphoreType.DMA((2, WT_PARTS)),
            pltpu.SemaphoreType.DMA((2, n_in)),
            pltpu.SemaphoreType.DMA((2, 2)),
            pltpu.SemaphoreType.DMA((2,)),
            pltpu.SemaphoreType.DMA((2,)),
        ],
        input_output_aliases={4 + n_in + k: k for k in range(4)},
        compiler_params=params(SMALL),
        cost_estimate=cost(8 * width * h * OWN, 4 * width * h + 8 * OWN * (h + width)),
    )(info, labels, in_hbm(wt_p), in_hbm(wt_r), *[arr for arr, _, _, _ in pieces], *prev)


def merge_kernel(*refs):
    ins, out = refs[:-1], refs[-1]
    row = lambda ref, k: ref[:, k : k + 1]
    for top, sums in ((0, (1, 2, 3)), (4, (5,))):
        peak = functools.reduce(jnp.maximum, [row(ref, top) for ref in ins])
        scale = [jnp.exp(row(ref, top) - peak) for ref in ins]
        out[:, top : top + 1] = peak
        for k in sums:
            out[:, k : k + 1] = sum(w * row(ref, k) for w, ref in zip(scale, ins))
    for k in (6, 7):
        out[:, k : k + 1] = sum(row(ref, k) for ref in ins)


def merge(*stats):
    return pl.pallas_call(
        merge_kernel,
        out_shape=jax.ShapeDtypeStruct(stats[0].shape, F32),
        compiler_params=params(),
        cost_estimate=cost(10 * stats[0].size * len(stats), 4 * stats[0].size * (len(stats) + 1)),
    )(*stats)


def by_xor(n, k):
    return [(i, i ^ k) for i in range(n)]


def by_shift(n, k):
    return [(i, (i + k) % n) for i in range(n)]


def all_merge(stats):
    for axis, n, rounds in (
        ("core", NC, (by_xor(NC, 1),)),
        ("x", NX, (by_xor(NX, 1), by_xor(NX, 3))),
        ("y", NY, (by_xor(NY, 1), by_xor(NY, 3))),
        ("z", NZ, (by_xor(NZ, 1), by_xor(NZ, 2), [(i, ((6 if i % 2 == 0 else 8) - i) % NZ) for i in range(NZ)])),
    ):
        for pairs in rounds:
            stats = merge(stats, lax.ppermute(stats, axis, pairs))
    return stats


def row_results(st):
    lse_z = st[0:1] + jnp.log(st[1:2])
    lse_r = st[4:5] + jnp.log(st[5:6])
    entropy = lse_z - st[2:3] / st[1:2]
    kl = (st[2:3] - st[3:4]) / st[1:2] - lse_z + lse_r
    return lse_z, lse_r, entropy, kl


def grad_of(z, r, ids, adv, st, first):
    col = (lax.broadcasted_iota(I32, z.shape, 0) + first).astype(F32)
    lse_z, lse_r, entropy, kl = row_results(st)
    lp = z - lse_z
    lq = r - lse_r
    p = jnp.exp(lp)
    hot = jnp.where(col == ids, 1.0, 0.0)
    return (-adv * (hot - p) + 0.1 * p * (lp - lq - kl) + 0.05 * p * (lp + entropy)).astype(BF)


W_PARTS = 2


def w_loads(y, w_hbm, wb, sem):
    return [
        pltpu.make_async_copy(w_hbm.at[y, pl.ds(k, m)], wb.at[y, pl.ds(k, m)], sem.at[y, i])
        for i, (k, m) in enumerate(split(wb.shape[1], W_PARTS))
    ]


def term_loop(info_ref, base, load_w, wb, rows_of, far_ref, near_ref):
    def step(y, _):
        for copy in load_w(y):
            copy.wait()
        rows = jnp.concatenate([rows_of(x) for x in range(NX)], axis=1)
        acc = jnp.dot(wb[y], rows, preferred_element_type=F32).astype(BF)
        for x in range(NX):
            at = base + 2 * (y * NX + x)
            group, k = info_ref[at], info_ref[at + 1]

            @pl.when(group == 0)
            def _():
                far_ref[k] = acc[:, x * OWN : (x + 1) * OWN]

            @pl.when(group > 0)
            def _():
                near_ref[group - 1, k] = acc[:, x * OWN : (x + 1) * OWN]

        return 0

    lax.fori_loop(0, NY, step, 0)


def grad_term_kernel(info_ref, lab_ref, st_ref, z_hbm, r_hbm, w_hbm, g_hbm, far_ref, near_ref, zb, rb, wb, gb, in_sem, w_sem, g_sem):
    n = zb.shape[0]

    def load(k):
        return (
            pltpu.make_async_copy(z_hbm.at[k], zb.at[k], in_sem.at[0, k]),
            pltpu.make_async_copy(r_hbm.at[k], rb.at[k], in_sem.at[1, k]),
        )

    def load_w(y):
        return w_loads(y, w_hbm, wb, w_sem)

    def store(k):
        return pltpu.make_async_copy(gb.at[k], g_hbm.at[k], g_sem.at[k])

    for k in range(n):
        for copy in load(k):
            copy.start()

    def step(k, _):
        for copy in load(k):
            copy.wait()

        @pl.when(k < NY)
        def _():
            for copy in load_w(k):
                copy.start()

        gb[k] = grad_of(zb[k], rb[k], lab_ref[k, 0:1], lab_ref[k, 1:2], st_ref[k], info_ref[0])
        store(k).start()
        return 0

    lax.fori_loop(0, n, step, 0)
    term_loop(info_ref, 2, load_w, wb, lambda x: gb[info_ref[1] * NX + x], far_ref, near_ref)
    for k in range(n):
        store(k).wait()


def own_term_kernel(info_ref, w_hbm, g_hbm, far_ref, near_ref, wb, gb, w_sem, g_sem):
    def load_w(y):
        return w_loads(y, w_hbm, wb, w_sem)

    def load_g(x):
        return pltpu.make_async_copy(g_hbm.at[info_ref[0] * NX + x], gb.at[x], g_sem.at[x])

    for x in range(NX):
        load_g(x).start()
    for y in range(NY):
        for copy in load_w(y):
            copy.start()
    for x in range(NX):
        load_g(x).wait()
    term_loop(info_ref, 1, load_w, wb, lambda x: gb[x], far_ref, near_ref)


def term_places(to_x, ix, iy):
    out = []
    for y in range(NY):
        for x in range(NX):
            distance = jnp.where(to_x, x - ix, y - iy) % NX
            group = jnp.where(distance == 0, 3, jnp.where(distance == 1, 1, jnp.where(distance == 2, 0, 2)))
            out += [group, jnp.where(to_x, y, x)]
    return out


def pack(values):
    return jnp.stack([jnp.asarray(v, I32) for v in values])


def term_shapes(m):
    return [jax.ShapeDtypeStruct((NX, m, OWN), BF), jax.ShapeDtypeStruct((NX - 1, NX, m, OWN), BF)]


def grad_and_terms(first, core, places, labels, stats, z, r, w):
    n, width, _ = z.shape
    m = w.shape[1]
    hbm, vmem = pl.BlockSpec(memory_space=pl.ANY), pl.BlockSpec(memory_space=VMEM)
    return pl.pallas_call(
        grad_term_kernel,
        out_shape=[HBM(z.shape, BF)] + term_shapes(m),
        in_specs=[pl.BlockSpec(memory_space=SMEM), vmem, vmem, hbm, hbm, hbm],
        out_specs=[hbm, vmem, vmem],
        scratch_shapes=[
            VMEM(z.shape, F32),
            VMEM(z.shape, F32),
            VMEM(w.shape, BF),
            VMEM(z.shape, BF),
            pltpu.SemaphoreType.DMA((2, n)),
            pltpu.SemaphoreType.DMA((NY, W_PARTS)),
            pltpu.SemaphoreType.DMA((n,)),
        ],
        compiler_params=params(),
        cost_estimate=cost(2 * w.size * NX * OWN + 16 * z.size, 10 * z.size + 2 * w.size + 8 * m * NX * OWN, z.size),
    )(pack([first, core] + places), labels, stats, in_hbm(z), in_hbm(r), in_hbm(w))


def own_terms(core, places, g, w):
    m, width = w.shape[1:]
    hbm, vmem = pl.BlockSpec(memory_space=pl.ANY), pl.BlockSpec(memory_space=VMEM)
    return pl.pallas_call(
        own_term_kernel,
        out_shape=term_shapes(m),
        in_specs=[pl.BlockSpec(memory_space=SMEM), hbm, hbm],
        out_specs=[vmem, vmem],
        scratch_shapes=[
            VMEM(w.shape, BF),
            VMEM((NX, width, OWN), BF),
            pltpu.SemaphoreType.DMA((NY, W_PARTS)),
            pltpu.SemaphoreType.DMA((NX,)),
        ],
        compiler_params=params(),
        cost_estimate=cost(2 * w.size * NX * OWN, 2 * w.size + g.size + 8 * m * NX * OWN),
    )(pack([core] + places), in_hbm(w), in_hbm(g))


def d_policy_kernel(first, x_hbm, g_hbm, out_hbm, xb, gb, ob, x_sem, g_sem, o_sem):
    tiles, _, m, _ = xb.shape

    def rows(t):
        return pl.ds(pl.multiple_of(first + t * m, 16), m)

    n = gb.shape[0]

    def load(t):
        return pltpu.make_async_copy(x_hbm.at[:, rows(t)], xb.at[t], x_sem.at[t])

    def store(t):
        return pltpu.make_async_copy(ob.at[t], out_hbm.at[rows(t)], o_sem.at[t])

    load_g = [pltpu.make_async_copy(g_hbm.at[b], gb.at[b], g_sem.at[b]) for b in range(n)]
    for copy in load_g:
        copy.start()
    for t in range(tiles):
        load(t).start()
    for copy in load_g:
        copy.wait()

    def step(t, _):
        load(t).wait()
        acc = 0.0
        for j in range(0, NX * NC, 2):
            lhs = jnp.concatenate((xb[t, j], xb[t, j + 1]), axis=1)
            rhs = jnp.concatenate((gb[j], gb[j + 1]), axis=1)
            acc = acc + lax.dot_general(lhs, rhs, (((1,), (1,)), ((), ())), preferred_element_type=F32)
        ob[t] = acc.astype(BF)
        store(t).start()
        return 0

    lax.fori_loop(0, tiles, step, 0)
    for t in range(tiles):
        store(t).wait()


def d_policy_half(x, g, first, prev=None):
    n, h, _ = x.shape
    width = g.shape[1]
    tiles = 3
    m = h // 2 // tiles
    hbm = pl.BlockSpec(memory_space=pl.ANY)
    body = functools.partial(d_policy_kernel, first)
    if prev is not None:
        inner = body

        def body(x_hbm, g_hbm, _, *refs):
            inner(x_hbm, g_hbm, *refs)

    return pl.pallas_call(
        body,
        out_shape=HBM((h, width), BF),
        in_specs=[hbm, hbm] + ([hbm] if prev is not None else []),
        out_specs=hbm,
        scratch_shapes=[
            VMEM((tiles, n, m, OWN), BF),
            VMEM(g.shape, BF),
            VMEM((tiles, m, width), BF),
            pltpu.SemaphoreType.DMA((tiles,)),
            pltpu.SemaphoreType.DMA((n,)),
            pltpu.SemaphoreType.DMA((tiles,)),
        ],
        input_output_aliases={} if prev is None else {2: 0},
        compiler_params=params(SMALL),
        cost_estimate=cost(h * width * n * OWN, x.size + 2 * g.size + h * width),
    )(in_hbm(x), in_hbm(g), *([] if prev is None else [in_hbm(prev)]))


UP_X, DOWN_X = by_shift(NX, 1), by_shift(NX, NX - 1)
UP_Y, DOWN_Y = by_shift(NY, 1), by_shift(NY, NY - 1)
ALL = ("x", "core", "z", "y")


def swap(a):
    return lax.ppermute(a, "core", by_xor(NC, 1))


def cut(a, first, n):
    return lax.dynamic_slice_in_dim(a, first, n, 0)


def core_route(d, second):
    pairs = []
    for x in range(NX):
        for c in range(NC):
            for z in range(NZ):
                for y in range(NY):
                    along_x = (c == 0) != second
                    x2, y2 = ((x + d) % NX, y) if along_x else (x, (y + d) % NY)
                    pairs.append((((x * NC + c) * NZ + z) * NY + y, ((x2 * NC + c) * NZ + z) * NY + y2))
    return pairs


def label_rows(ids, adv):
    top = lax.reduce_precision(adv, 8, 7)
    middle = lax.reduce_precision(adv - top, 8, 7)
    parts = [(ids >> 12).astype(F32), ((ids >> 6) & 63).astype(F32), (ids & 63).astype(F32), top, middle, adv - top - middle]
    return jnp.pad(jnp.stack(parts).astype(BF), ((0, 10), (0, 0)))


def add(a, b):
    return (a.astype(F32) + b.astype(F32)).astype(BF)


def after(value, *first):
    return lax.optimization_barrier((value, *first))[0]


def shards(hidden, ref_hidden, sampled, advantage, policy_head, ref_head):
    ix, ic, iz, iy = (lax.axis_index(a) for a in ALL)
    h, width = policy_head.shape
    half, quarter = h // 2, h // 4
    odd = iy % 2
    lo, hi, skip = odd * half, (1 - odd) * half, odd * quarter
    piece = h // (NZ * NY)
    padded = -(-piece // 16) * 16

    def block(d, other):
        return (ic ^ other) * NX + (ix + d) % NX

    own_p, own_r = hidden.T, ref_hidden.T
    marks = label_rows(sampled, advantage)
    a_p = lax.ppermute(jnp.concatenate((cut(own_p, lo, half), marks), axis=0), "x", DOWN_X)
    b_p = lax.ppermute(jnp.concatenate((cut(own_p, hi, half), marks), axis=0), "x", UP_X)
    a_r = lax.ppermute(cut(own_r, lo, half), "x", DOWN_X)
    b_r = lax.ppermute(cut(own_r, hi, half), "x", UP_X)

    wt_p, w_yz = prep(policy_head, padded)
    w_yz = w_yz.reshape(NY, NZ * padded, width)
    (wt_r,) = prep(after(ref_head, wt_p))
    a_p, b_p, wt_p, wt_r = lax.optimization_barrier((a_p, b_p, wt_p, wt_r))
    a2_p = lax.ppermute(a_p, "y", UP_Y)
    b2_p = lax.ppermute(b_p, "y", DOWN_Y)
    there = [swap(arr) for arr in (own_p, a_p, b_p)]
    a_r, b_r, *there = lax.optimization_barrier((a_r, b_r, *there))
    c = lax.ppermute(jnp.concatenate((cut(a_p, skip, quarter), cut(a_r, skip, quarter), a_p[half:]), axis=0), "x", DOWN_X)
    d = lax.ppermute(jnp.concatenate((cut(b_p, skip, quarter), cut(b_r, skip, quarter), b_p[half:]), axis=0), "x", UP_X)
    a2_r = lax.ppermute(a_r, "y", UP_Y)
    b2_r = lax.ppermute(b_r, "y", DOWN_Y)
    rest = quarter - skip
    there += [swap(a2_p), swap(b2_p)]

    def early(here, there):
        out = []
        for k, (slot, f, rows) in enumerate(((0, 0, h), (2, lo, half), (4, hi, half), (2, hi, half), (4, lo, half))):
            out += [(here[k], slot, f, rows), (there[k], slot + 1, f, rows)]
        return out

    blocks = [block(dist, s) for dist in (0, 1, 3) for s in (0, 1)]
    z, x_all = head_product(wt_p, early((own_p, a_p, b_p, a2_p, b2_p), there), blocks, keep=True)
    c, d, z = lax.optimization_barrier((c, d, z))
    c2 = lax.ppermute(c, "y", UP_Y)
    d2 = lax.ppermute(d, "y", DOWN_Y)
    here_r = (own_r, a_r, b_r, a2_r, b2_r)
    there_r = [swap(after(arr, z)) for arr in here_r]
    (r,) = head_product(wt_r, early(here_r, there_r), blocks, keep=False)
    c2, d2, r = lax.optimization_barrier((c2, d2, r))

    last = (c, d, c2, d2)
    last_there = [swap(arr) for arr in last]
    marks = jnp.stack((marks, a_p[half:], c[2 * quarter :], b_p[half:]))
    marks = jnp.stack((marks, jnp.stack((swap(marks[0]), there[1][half:], last_there[0][2 * quarter :], there[2][half:]))))
    marks = marks[:, :, :6].astype(F32)
    labels = jnp.stack((marks[:, :, 0] * 4096.0 + marks[:, :, 1] * 64.0 + marks[:, :, 2], marks[:, :, 3] + marks[:, :, 4] + marks[:, :, 5]), axis=2)
    labels = jnp.where(ic == 0, labels, labels[::-1])
    labels = jnp.concatenate((labels, labels), axis=1)
    labels = lax.dynamic_slice_in_dim(labels, NX - ix, NX, 1).reshape(NC * NX, 2, OWN)

    first = ((((ix * NC + ic) * NZ + iz) * NY + iy) * width).astype(I32)
    stats = row_stats(first, blocks, z, r, labels)
    late = []
    for arr, arr_there, f in zip(last, last_there, (lo + skip, hi + skip, hi + rest, lo + rest)):
        late += [(arr, 0, f, quarter), (arr_there, 1, f, quarter)]
    z, r, x_all, stats = late_product(first, labels, wt_p, wt_r, late, [block(2, s) for s in (0, 1)], z, r, x_all, stats)

    stats = all_merge(stats)
    g, far_other, near_other = grad_and_terms(first, 1 - ic, term_places(ic == 1, ix, iy), labels, stats, z, r, w_yz)
    far_mine, near_mine = own_terms(ic, term_places(ic == 0, ix, iy), g, w_yz)
    far_other = swap(far_other)
    near_other = swap(near_other)
    far = add(far_mine, far_other)
    via_up = lax.ppermute(far[:2], ALL, core_route(1, False))
    via_down = lax.ppermute(far[2:], ALL, core_route(-1, False))
    d_policy = d_policy_half(x_all, after(g, far), 0)
    via_up, via_down, d_policy = lax.optimization_barrier((via_up, via_down, d_policy))
    near = near_mine.astype(F32) + near_other.astype(F32)
    to_up = jnp.concatenate(((near[0, :2] + via_up.astype(F32)).astype(BF), near[0, 2:].astype(BF)), axis=0)
    to_down = jnp.concatenate((near[1, :2].astype(BF), (near[1, 2:] + via_down.astype(F32)).astype(BF)), axis=0)
    from_down = lax.ppermute(to_up, ALL, core_route(1, False))
    from_up = lax.ppermute(to_down, ALL, core_route(-1, False))
    d_policy = d_policy_half(x_all, after(g, to_up, to_down), h // 2, d_policy)
    from_down, from_up, d_policy = lax.optimization_barrier((from_down, from_up, d_policy))
    parts = near[2] + from_down.astype(F32) + from_up.astype(F32)

    at = jnp.where(ic == 0, iy, ix)
    total = lax.dynamic_index_in_dim(parts, at, 0, keepdims=False)
    parts = parts.astype(BF)
    for dist in (1, 3, 2):
        part = lax.dynamic_index_in_dim(parts, (at + dist) % NX, 0, keepdims=False)
        total = total + lax.ppermute(part, ALL, core_route(dist, True)).astype(F32)
    total = total.astype(BF).reshape(NZ, padded, OWN)
    got = lax.all_to_all(total, "z", split_axis=0, concat_axis=0, tiled=True)
    d_hidden = jnp.sum(got.astype(F32), axis=0)[:piece].T

    mine = lax.dynamic_index_in_dim(stats, block(0, 0), 0, keepdims=False)
    lse_z, _, entropy, kl = row_results(mine)
    return (mine[6] - lse_z[0], entropy[0], kl[0], d_hidden, d_policy)


def solution(mesh):
    fine = Mesh(mesh.devices.reshape(NX, NC, NZ, NY), ("x", "core", "z", "y"))
    dp, vocab = ("x", "core"), ("z", "y")
    everybody = dp + vocab
    in_specs = (P(dp, None), P(dp, None), P(dp), P(dp), P(None, everybody), P(None, everybody))
    out_specs = (P(dp), P(dp), P(dp), P(dp, vocab), P(None, everybody))
    return jax.shard_map(shards, mesh=fine, in_specs=in_specs, out_specs=out_specs, check_vma=False)
```

```python
import functools

import jax
import jax.numpy as jnp
from jax import lax
from jax.experimental import pallas as pl
from jax.experimental.pallas import tpu as pltpu
from jax.sharding import Mesh, PartitionSpec as P

NX, NC, NZ, NY = 4, 2, 8, 4
OWN = 128
BF, F32, I32 = jnp.bfloat16, jnp.float32, jnp.int32
LIMIT, SMALL = 24 * 1024 * 1024, 16 * 1024 * 1024
VMEM, SMEM, HBM = pltpu.VMEM, pltpu.SMEM, pltpu.HBM


def params(limit=LIMIT):
    return pltpu.CompilerParams(vmem_limit_bytes=limit)


def in_hbm(a):
    return pltpu.with_memory_space_constraint(a, HBM)


def split(n, parts):
    step = -(-n // (16 * parts)) * 16
    return [(k, min(step, n - k)) for k in range(0, n, step)]


def cost(flops, nbytes, trans=0):
    return pl.CostEstimate(flops=int(flops), bytes_accessed=int(nbytes), transcendentals=int(trans))


def lanes(s):
    return pl.ds(pl.multiple_of(s * OWN, OWN), OWN)


def prep_kernel(piece, n_out, w_hbm, *refs):
    wt_hbm, wr_hbm = refs[0], refs[1 if n_out == 2 else 0]
    wbuf, tbuf, rbuf, in_sem, t_sem, r_sem = refs[n_out:]
    n, h, _ = wbuf.shape

    def load(s):
        return [
            pltpu.make_async_copy(w_hbm.at[pl.ds(k, m), lanes(s)], wbuf.at[s, pl.ds(k, m)], in_sem.at[s, i])
            for i, (k, m) in enumerate(split(h, 4))
        ]

    def store(s):
        copies = []
        for i, (k, m) in enumerate(split(OWN, 4)):
            rows = pl.ds(pl.multiple_of(s * OWN + k, 16), m)
            copies.append(pltpu.make_async_copy(tbuf.at[s, pl.ds(k, m)], wt_hbm.at[rows], t_sem.at[s, i]))
        if n_out == 2:
            for y in range(NY):
                copies.append(pltpu.make_async_copy(rbuf.at[s, y], wr_hbm.at[y, :, :, lanes(s)], r_sem.at[s, y]))
        return copies

    for s in range(n):
        for copy in load(s):
            copy.start()

    def step(s, _):
        for copy in load(s):
            copy.wait()
        w = wbuf[s]
        tbuf[s] = w.T
        if n_out == 2:
            fill = jnp.zeros((rbuf.shape[3] - piece, OWN), w.dtype)
            for z in range(NZ):
                for y in range(NY):
                    k = (z * NY + y) * piece
                    rbuf[s, y, z] = jnp.concatenate((w[k : k + piece], fill), axis=0)
        for copy in store(s):
            copy.start()
        return 0

    lax.fori_loop(0, n, step, 0)
    for s in range(n):
        for copy in store(s):
            copy.wait()


def prep(w, padded=None):
    h, width = w.shape
    n = width // OWN
    out_shape = [HBM((width, h), BF)]
    if padded:
        out_shape.append(HBM((NY, NZ, padded, width), BF))
    return pl.pallas_call(
        functools.partial(prep_kernel, h // (NZ * NY), len(out_shape)),
        out_shape=out_shape,
        in_specs=[pl.BlockSpec(memory_space=pl.ANY)],
        out_specs=[pl.BlockSpec(memory_space=pl.ANY)] * len(out_shape),
        scratch_shapes=[
            VMEM((n, h, OWN), BF),
            VMEM((n, OWN, h), BF),
            VMEM((n if padded else 1, NY, NZ, padded or 16, OWN), BF),
            pltpu.SemaphoreType.DMA((n, 4)),
            pltpu.SemaphoreType.DMA((n, 4)),
            pltpu.SemaphoreType.DMA((n, NY)),
        ],
        compiler_params=params(SMALL),
        cost_estimate=cost(0, 6 * h * width),
    )(in_hbm(w))


WT_PARTS = 8


def wt_loads(src, dst, sem):
    return [
        pltpu.make_async_copy(src.at[pl.ds(k, m)], dst.at[pl.ds(k, m)], sem.at[i])
        for i, (k, m) in enumerate(split(src.shape[0], WT_PARTS))
    ]


def head_kernel(plan, slots, n_in, n_prev, n_out, info_ref, wt_hbm, *refs):
    arrays = refs[:n_in]
    outs = refs[n_in + n_prev : n_in + n_prev + n_out]
    wt, xs, obuf, wt_sem, in_sem, out_sem, keep_sem = refs[n_in + n_prev + n_out :]
    wt_copies = wt_loads(wt_hbm, wt, wt_sem)
    for copy in wt_copies:
        copy.start()
    copies = []
    for i, (at, slot, rows) in enumerate(plan):
        first = pl.multiple_of(info_ref[slots + i], 16)
        src = arrays[at].at[pl.ds(0, rows)]
        copy = pltpu.make_async_copy(src, xs.at[pl.ds(first, rows), pl.ds(slot * OWN, OWN)], in_sem.at[i])
        copy.start()
        copies.append(copy)
    for copy in copies:
        copy.wait()
    done = []
    if n_out == 2:
        for s in range(slots):
            copy = pltpu.make_async_copy(xs.at[:, pl.ds(s * OWN, OWN)], outs[1].at[info_ref[s]], keep_sem.at[s])
            copy.start()
            done.append(copy)
    for copy in wt_copies:
        copy.wait()
    width = wt.shape[0]
    tile = width // 2

    def step(t, _):
        rows = pl.ds(pl.multiple_of(t * tile, tile), tile)
        acc = jnp.dot(wt[rows, :], xs[...], preferred_element_type=F32)
        for s in range(slots):
            obuf[s, rows, :] = acc[:, s * OWN : (s + 1) * OWN]
        return 0

    lax.fori_loop(0, width // tile, step, 0)
    for s in range(slots):
        copy = pltpu.make_async_copy(obuf.at[s], outs[0].at[info_ref[s]], out_sem.at[s])
        copy.start()
        done.append(copy)
    for copy in done:
        copy.wait()


def head_product(wt, pieces, slot_blocks, keep, prev=()):
    width, h = wt.shape
    slots = len(slot_blocks)
    arrays = [arr for arr, _, _, _ in pieces]
    plan = [(i, slot, rows) for i, (_, slot, _, rows) in enumerate(pieces)]
    info = jnp.stack([jnp.asarray(v, I32) for v in slot_blocks] + [jnp.asarray(f, I32) for _, _, f, _ in pieces])
    out_shape = [HBM((NX * NC, width, OWN), F32)]
    if keep:
        out_shape.append(HBM((NX * NC, h, OWN), BF))
    any_spec = pl.BlockSpec(memory_space=pl.ANY)
    n_in = len(arrays)
    return pl.pallas_call(
        functools.partial(head_kernel, plan, slots, n_in, len(prev), len(out_shape)),
        out_shape=out_shape,
        in_specs=[pl.BlockSpec(memory_space=SMEM)] + [any_spec] * (1 + n_in + len(prev)),
        out_specs=[any_spec] * len(out_shape),
        scratch_shapes=[
            VMEM((width, h), BF),
            VMEM((h, slots * OWN), BF),
            VMEM((slots, width, OWN), F32),
            pltpu.SemaphoreType.DMA((WT_PARTS,)),
            pltpu.SemaphoreType.DMA((len(plan),)),
            pltpu.SemaphoreType.DMA((slots,)),
            pltpu.SemaphoreType.DMA((slots,)),
        ],
        input_output_aliases={2 + n_in + k: k for k in range(len(prev))},
        compiler_params=params(SMALL),
        cost_estimate=cost(2 * width * h * slots * OWN, width * h * 2 + slots * OWN * (h * 2 + width * 4)),
    )(info, in_hbm(wt), *arrays, *prev)


def stats_rows(z, r, ids, first):
    col = (lax.broadcasted_iota(I32, z.shape, 0) + first).astype(F32)
    m_z = jnp.max(z, axis=0, keepdims=True)
    m_r = jnp.max(r, axis=0, keepdims=True)
    e = jnp.exp(z - m_z)
    rows = (
        m_z,
        jnp.sum(e, axis=0, keepdims=True),
        jnp.sum(e * z, axis=0, keepdims=True),
        jnp.sum(e * r, axis=0, keepdims=True),
        m_r,
        jnp.sum(jnp.exp(r - m_r), axis=0, keepdims=True),
        jnp.sum(jnp.where(col == ids, z, 0.0), axis=0, keepdims=True),
        jnp.zeros_like(m_z),
    )
    return jnp.concatenate(rows, axis=0)


def stats_kernel(n, info_ref, lab_ref, z_hbm, r_hbm, out_ref, zb, rb, sem):
    def load(k):
        at = info_ref[k + 1]
        return (
            pltpu.make_async_copy(z_hbm.at[at], zb.at[k], sem.at[0, k]),
            pltpu.make_async_copy(r_hbm.at[at], rb.at[k], sem.at[1, k]),
        )

    for k in range(n):
        for copy in load(k):
            copy.start()

    def step(k, _):
        for copy in load(k):
            copy.wait()
        at = info_ref[k + 1]
        out_ref[at] = stats_rows(zb[k], rb[k], lab_ref[at, 0:1], info_ref[0])
        return 0

    lax.fori_loop(0, n, step, 0)


def row_stats(first, blocks, z, r, labels):
    width, n = z.shape[1], len(blocks)
    info = jnp.stack([first] + [jnp.asarray(b, I32) for b in blocks])
    return pl.pallas_call(
        functools.partial(stats_kernel, n),
        out_shape=jax.ShapeDtypeStruct((z.shape[0], 8, OWN), F32),
        in_specs=[pl.BlockSpec(memory_space=SMEM), pl.BlockSpec(memory_space=VMEM)] + [pl.BlockSpec(memory_space=pl.ANY)] * 2,
        out_specs=pl.BlockSpec(memory_space=VMEM),
        scratch_shapes=[VMEM((n, width, OWN), F32), VMEM((n, width, OWN), F32), pltpu.SemaphoreType.DMA((2, n))],
        compiler_params=params(SMALL),
        cost_estimate=cost(12 * z.size, 6 * z.size, 2 * z.size),
    )(info, labels, in_hbm(z), in_hbm(r))


def late_kernel(plan, n_in, info_ref, lab_ref, wp_hbm, wr_hbm, *refs):
    arrays = refs[:n_in]
    z_out, r_out, x_out, st_out = refs[n_in + 4 : n_in + 8]
    wts, xs, obuf, stbuf, wt_sem, in_sem, out_sem, keep_sem, st_sem = refs[n_in + 8 :]
    wt_copies = [wt_loads(w, wts.at[k], wt_sem.at[k]) for k, w in enumerate((wp_hbm, wr_hbm))]
    copies = [[], []]
    for head in range(2):
        for copy in wt_copies[head]:
            copy.start()
        for i, (at, slot, rows) in enumerate(plan):
            first = pl.multiple_of(info_ref[3 + i], 16)
            dst = xs.at[head, pl.ds(first, rows), pl.ds(slot * OWN, OWN)]
            copy = pltpu.make_async_copy(arrays[at].at[pl.ds(head * rows, rows)], dst, in_sem.at[head, i])
            copy.start()
            copies[head].append(copy)
    width = wts.shape[1]
    tile = width // 2
    done = []
    for head, out in enumerate((z_out, r_out)):
        for copy in copies[head]:
            copy.wait()
        for copy in wt_copies[head]:
            copy.wait()

        def step(t, _):
            rows = pl.ds(pl.multiple_of(t * tile, tile), tile)
            acc = jnp.dot(wts[head, rows, :], xs[head], preferred_element_type=F32)
            for s in range(2):
                obuf[head, s, rows, :] = acc[:, s * OWN : (s + 1) * OWN]
            return 0

        lax.fori_loop(0, width // tile, step, 0)
        for s in range(2):
            copy = pltpu.make_async_copy(obuf.at[head, s], out.at[info_ref[1 + s]], out_sem.at[head, s])
            copy.start()
            done.append(copy)
            if head == 0:
                copy = pltpu.make_async_copy(xs.at[0, :, pl.ds(s * OWN, OWN)], x_out.at[info_ref[1 + s]], keep_sem.at[s])
                copy.start()
                done.append(copy)
    for s in range(2):
        stbuf[s] = stats_rows(obuf[0, s], obuf[1, s], lab_ref[info_ref[1 + s], 0:1], info_ref[0])
        copy = pltpu.make_async_copy(stbuf.at[s], st_out.at[info_ref[1 + s]], st_sem.at[s])
        copy.start()
        done.append(copy)
    for copy in done:
        copy.wait()


def late_product(first, labels, wt_p, wt_r, pieces, blocks, z, r, x_all, stats):
    width, h = wt_p.shape
    plan = [(i, slot, rows) for i, (_, slot, _, rows) in enumerate(pieces)]
    info = jnp.stack([first] + [jnp.asarray(v, I32) for v in blocks] + [jnp.asarray(f, I32) for _, _, f, _ in pieces])
    n_in = len(pieces)
    hbm = pl.BlockSpec(memory_space=pl.ANY)
    prev = [in_hbm(a) for a in (z, r, x_all, stats)]
    return pl.pallas_call(
        functools.partial(late_kernel, plan, n_in),
        out_shape=[HBM(a.shape, a.dtype) for a in prev],
        in_specs=[pl.BlockSpec(memory_space=SMEM), pl.BlockSpec(memory_space=VMEM)] + [hbm] * (2 + n_in + 4),
        out_specs=[hbm] * 4,
        scratch_shapes=[
            VMEM((2, width, h), BF),
            VMEM((2, h, 2 * OWN), BF),
            VMEM((2, 2, width, OWN), F32),
            VMEM((2, 8, OWN), F32),
            pltpu.SemaphoreType.DMA((2, WT_PARTS)),
            pltpu.SemaphoreType.DMA((2, n_in)),
            pltpu.SemaphoreType.DMA((2, 2)),
            pltpu.SemaphoreType.DMA((2,)),
            pltpu.SemaphoreType.DMA((2,)),
        ],
        input_output_aliases={4 + n_in + k: k for k in range(4)},
        compiler_params=params(SMALL),
        cost_estimate=cost(8 * width * h * OWN, 4 * width * h + 8 * OWN * (h + width)),
    )(info, labels, in_hbm(wt_p), in_hbm(wt_r), *[arr for arr, _, _, _ in pieces], *prev)


def merge_kernel(*refs):
    ins, out = refs[:-1], refs[-1]
    row = lambda ref, k: ref[:, k : k + 1]
    for top, sums in ((0, (1, 2, 3)), (4, (5,))):
        peak = functools.reduce(jnp.maximum, [row(ref, top) for ref in ins])
        scale = [jnp.exp(row(ref, top) - peak) for ref in ins]
        out[:, top : top + 1] = peak
        for k in sums:
            out[:, k : k + 1] = sum(w * row(ref, k) for w, ref in zip(scale, ins))
    for k in (6, 7):
        out[:, k : k + 1] = sum(row(ref, k) for ref in ins)


def merge(*stats):
    return pl.pallas_call(
        merge_kernel,
        out_shape=jax.ShapeDtypeStruct(stats[0].shape, F32),
        compiler_params=params(),
        cost_estimate=cost(10 * stats[0].size * len(stats), 4 * stats[0].size * (len(stats) + 1)),
    )(*stats)


def by_xor(n, k):
    return [(i, i ^ k) for i in range(n)]


def by_shift(n, k):
    return [(i, (i + k) % n) for i in range(n)]


def all_merge(stats):
    for axis, n, rounds in (
        ("core", NC, (by_xor(NC, 1),)),
        ("x", NX, (by_xor(NX, 1), by_xor(NX, 3))),
        ("y", NY, (by_xor(NY, 1), by_xor(NY, 3))),
        ("z", NZ, (by_xor(NZ, 1), by_xor(NZ, 2), [(i, ((6 if i % 2 == 0 else 8) - i) % NZ) for i in range(NZ)])),
    ):
        for pairs in rounds:
            stats = merge(stats, lax.ppermute(stats, axis, pairs))
    return stats


def row_results(st):
    lse_z = st[0:1] + jnp.log(st[1:2])
    lse_r = st[4:5] + jnp.log(st[5:6])
    entropy = lse_z - st[2:3] / st[1:2]
    kl = (st[2:3] - st[3:4]) / st[1:2] - lse_z + lse_r
    return lse_z, lse_r, entropy, kl


def grad_of(z, r, ids, adv, st, first):
    col = (lax.broadcasted_iota(I32, z.shape, 0) + first).astype(F32)
    lse_z, lse_r, entropy, kl = row_results(st)
    lp = z - lse_z
    lq = r - lse_r
    p = jnp.exp(lp)
    hot = jnp.where(col == ids, 1.0, 0.0)
    return (-adv * (hot - p) + 0.1 * p * (lp - lq - kl) + 0.05 * p * (lp + entropy)).astype(BF)


W_PARTS = 2


def w_loads(y, w_hbm, wb, sem):
    return [
        pltpu.make_async_copy(w_hbm.at[y, pl.ds(k, m)], wb.at[y, pl.ds(k, m)], sem.at[y, i])
        for i, (k, m) in enumerate(split(wb.shape[1], W_PARTS))
    ]


def term_loop(info_ref, base, load_w, wb, rows_of, far_ref, near_ref):
    def step(y, _):
        for copy in load_w(y):
            copy.wait()
        rows = jnp.concatenate([rows_of(x) for x in range(NX)], axis=1)
        acc = jnp.dot(wb[y], rows, preferred_element_type=F32).astype(BF)
        for x in range(NX):
            at = base + 2 * (y * NX + x)
            group, k = info_ref[at], info_ref[at + 1]

            @pl.when(group == 0)
            def _():
                far_ref[k] = acc[:, x * OWN : (x + 1) * OWN]

            @pl.when(group > 0)
            def _():
                near_ref[group - 1, k] = acc[:, x * OWN : (x + 1) * OWN]

        return 0

    lax.fori_loop(0, NY, step, 0)


def grad_term_kernel(info_ref, lab_ref, st_ref, z_hbm, r_hbm, w_hbm, g_hbm, far_ref, near_ref, zb, rb, wb, gb, in_sem, w_sem, g_sem):
    n = zb.shape[0]

    def load(k):
        return (
            pltpu.make_async_copy(z_hbm.at[k], zb.at[k], in_sem.at[0, k]),
            pltpu.make_async_copy(r_hbm.at[k], rb.at[k], in_sem.at[1, k]),
        )

    def load_w(y):
        return w_loads(y, w_hbm, wb, w_sem)

    def store(k):
        return pltpu.make_async_copy(gb.at[k], g_hbm.at[k], g_sem.at[k])

    for k in range(n):
        for copy in load(k):
            copy.start()

    def step(k, _):
        for copy in load(k):
            copy.wait()

        @pl.when(k < NY)
        def _():
            for copy in load_w(k):
                copy.start()

        gb[k] = grad_of(zb[k], rb[k], lab_ref[k, 0:1], lab_ref[k, 1:2], st_ref[k], info_ref[0])
        store(k).start()
        return 0

    lax.fori_loop(0, n, step, 0)
    term_loop(info_ref, 2, load_w, wb, lambda x: gb[info_ref[1] * NX + x], far_ref, near_ref)
    for k in range(n):
        store(k).wait()


def own_term_kernel(info_ref, w_hbm, g_hbm, far_ref, near_ref, wb, gb, w_sem, g_sem):
    def load_w(y):
        return w_loads(y, w_hbm, wb, w_sem)

    def load_g(x):
        return pltpu.make_async_copy(g_hbm.at[info_ref[0] * NX + x], gb.at[x], g_sem.at[x])

    for x in range(NX):
        load_g(x).start()
    for y in range(NY):
        for copy in load_w(y):
            copy.start()
    for x in range(NX):
        load_g(x).wait()
    term_loop(info_ref, 1, load_w, wb, lambda x: gb[x], far_ref, near_ref)


def term_places(to_x, ix, iy):
    out = []
    for y in range(NY):
        for x in range(NX):
            distance = jnp.where(to_x, x - ix, y - iy) % NX
            group = jnp.where(distance == 0, 3, jnp.where(distance == 1, 1, jnp.where(distance == 2, 0, 2)))
            out += [group, jnp.where(to_x, y, x)]
    return out


def pack(values):
    return jnp.stack([jnp.asarray(v, I32) for v in values])


def term_shapes(m):
    return [jax.ShapeDtypeStruct((NX, m, OWN), BF), jax.ShapeDtypeStruct((NX - 1, NX, m, OWN), BF)]


def grad_and_terms(first, core, places, labels, stats, z, r, w):
    n, width, _ = z.shape
    m = w.shape[1]
    hbm, vmem = pl.BlockSpec(memory_space=pl.ANY), pl.BlockSpec(memory_space=VMEM)
    return pl.pallas_call(
        grad_term_kernel,
        out_shape=[HBM(z.shape, BF)] + term_shapes(m),
        in_specs=[pl.BlockSpec(memory_space=SMEM), vmem, vmem, hbm, hbm, hbm],
        out_specs=[hbm, vmem, vmem],
        scratch_shapes=[
            VMEM(z.shape, F32),
            VMEM(z.shape, F32),
            VMEM(w.shape, BF),
            VMEM(z.shape, BF),
            pltpu.SemaphoreType.DMA((2, n)),
            pltpu.SemaphoreType.DMA((NY, W_PARTS)),
            pltpu.SemaphoreType.DMA((n,)),
        ],
        compiler_params=params(),
        cost_estimate=cost(2 * w.size * NX * OWN + 16 * z.size, 10 * z.size + 2 * w.size + 8 * m * NX * OWN, z.size),
    )(pack([first, core] + places), labels, stats, in_hbm(z), in_hbm(r), in_hbm(w))


def own_terms(core, places, g, w):
    m, width = w.shape[1:]
    hbm, vmem = pl.BlockSpec(memory_space=pl.ANY), pl.BlockSpec(memory_space=VMEM)
    return pl.pallas_call(
        own_term_kernel,
        out_shape=term_shapes(m),
        in_specs=[pl.BlockSpec(memory_space=SMEM), hbm, hbm],
        out_specs=[vmem, vmem],
        scratch_shapes=[
            VMEM(w.shape, BF),
            VMEM((NX, width, OWN), BF),
            pltpu.SemaphoreType.DMA((NY, W_PARTS)),
            pltpu.SemaphoreType.DMA((NX,)),
        ],
        compiler_params=params(),
        cost_estimate=cost(2 * w.size * NX * OWN, 2 * w.size + g.size + 8 * m * NX * OWN),
    )(pack([core] + places), in_hbm(w), in_hbm(g))


def d_policy_kernel(x_hbm, g_hbm, out_hbm, xb, gb, ob, x_sem, g_sem, o_sem):
    tiles, _, m, _ = xb.shape

    def rows(t):
        return pl.ds(pl.multiple_of(t * m, 16), m)

    n = gb.shape[0]

    def load(t):
        return pltpu.make_async_copy(x_hbm.at[:, rows(t)], xb.at[t], x_sem.at[t])

    def store(t):
        return pltpu.make_async_copy(ob.at[t], out_hbm.at[rows(t)], o_sem.at[t])

    load_g = [pltpu.make_async_copy(g_hbm.at[b], gb.at[b], g_sem.at[b]) for b in range(n)]
    for copy in load_g:
        copy.start()
    for t in range(tiles):
        load(t).start()
    for copy in load_g:
        copy.wait()

    def step(t, _):
        load(t).wait()
        acc = 0.0
        for j in range(0, NX * NC, 2):
            lhs = jnp.concatenate((xb[t, j], xb[t, j + 1]), axis=1)
            rhs = jnp.concatenate((gb[j], gb[j + 1]), axis=1)
            acc = acc + lax.dot_general(lhs, rhs, (((1,), (1,)), ((), ())), preferred_element_type=F32)
        ob[t] = acc.astype(BF)
        store(t).start()
        return 0

    lax.fori_loop(0, tiles, step, 0)
    for t in range(tiles):
        store(t).wait()


def d_policy_of(x, g):
    n, h, _ = x.shape
    width = g.shape[1]
    tiles = 6
    m = h // tiles
    hbm = pl.BlockSpec(memory_space=pl.ANY)
    return pl.pallas_call(
        d_policy_kernel,
        out_shape=jax.ShapeDtypeStruct((h, width), BF),
        in_specs=[hbm, hbm],
        out_specs=hbm,
        scratch_shapes=[
            VMEM((tiles, n, m, OWN), BF),
            VMEM(g.shape, BF),
            VMEM((tiles, m, width), BF),
            pltpu.SemaphoreType.DMA((tiles,)),
            pltpu.SemaphoreType.DMA((n,)),
            pltpu.SemaphoreType.DMA((tiles,)),
        ],
        compiler_params=params(),
        cost_estimate=cost(2 * h * width * n * OWN, 2 * (x.size + g.size + h * width)),
    )(in_hbm(x), in_hbm(g))


UP_X, DOWN_X = by_shift(NX, 1), by_shift(NX, NX - 1)
UP_Y, DOWN_Y = by_shift(NY, 1), by_shift(NY, NY - 1)
ALL = ("x", "core", "z", "y")


def swap(a):
    return lax.ppermute(a, "core", by_xor(NC, 1))


def cut(a, first, n):
    return lax.dynamic_slice_in_dim(a, first, n, 0)


def core_route(d, second):
    pairs = []
    for x in range(NX):
        for c in range(NC):
            for z in range(NZ):
                for y in range(NY):
                    along_x = (c == 0) != second
                    x2, y2 = ((x + d) % NX, y) if along_x else (x, (y + d) % NY)
                    pairs.append((((x * NC + c) * NZ + z) * NY + y, ((x2 * NC + c) * NZ + z) * NY + y2))
    return pairs


def label_rows(ids, adv):
    top = lax.reduce_precision(adv, 8, 7)
    middle = lax.reduce_precision(adv - top, 8, 7)
    parts = [(ids >> 12).astype(F32), ((ids >> 6) & 63).astype(F32), (ids & 63).astype(F32), top, middle, adv - top - middle]
    return jnp.pad(jnp.stack(parts).astype(BF), ((0, 10), (0, 0)))


def add(a, b):
    return (a.astype(F32) + b.astype(F32)).astype(BF)


def after(value, *first):
    return lax.optimization_barrier((value, *first))[0]


def shards(hidden, ref_hidden, sampled, advantage, policy_head, ref_head):
    ix, ic, iz, iy = (lax.axis_index(a) for a in ALL)
    h, width = policy_head.shape
    half, quarter = h // 2, h // 4
    odd = iy % 2
    lo, hi, skip = odd * half, (1 - odd) * half, odd * quarter
    piece = h // (NZ * NY)
    padded = -(-piece // 16) * 16

    def block(d, other):
        return (ic ^ other) * NX + (ix + d) % NX

    own_p, own_r = hidden.T, ref_hidden.T
    marks = label_rows(sampled, advantage)
    a_p = lax.ppermute(jnp.concatenate((cut(own_p, lo, half), marks), axis=0), "x", DOWN_X)
    b_p = lax.ppermute(jnp.concatenate((cut(own_p, hi, half), marks), axis=0), "x", UP_X)
    a_r = lax.ppermute(cut(own_r, lo, half), "x", DOWN_X)
    b_r = lax.ppermute(cut(own_r, hi, half), "x", UP_X)

    wt_p, w_yz = prep(policy_head, padded)
    w_yz = w_yz.reshape(NY, NZ * padded, width)
    (wt_r,) = prep(after(ref_head, wt_p))
    a_p, b_p, wt_p, wt_r = lax.optimization_barrier((a_p, b_p, wt_p, wt_r))
    a2_p = lax.ppermute(a_p, "y", UP_Y)
    b2_p = lax.ppermute(b_p, "y", DOWN_Y)
    there = [swap(arr) for arr in (own_p, a_p, b_p)]
    a_r, b_r, *there = lax.optimization_barrier((a_r, b_r, *there))
    c = jnp.concatenate((cut(a_p, skip, quarter), cut(a_r, skip, quarter), a_p[half:]), axis=0)
    d = jnp.concatenate((cut(b_p, skip, quarter), cut(b_r, skip, quarter), b_p[half:]), axis=0)
    there += [swap(after(arr, c, d)) for arr in (a2_p, b2_p)]
    c = lax.ppermute(c, "x", DOWN_X)
    d = lax.ppermute(d, "x", UP_X)
    a2_r = lax.ppermute(a_r, "y", UP_Y)
    b2_r = lax.ppermute(b_r, "y", DOWN_Y)
    rest = quarter - skip

    def early(here, there):
        out = []
        for k, (slot, f, rows) in enumerate(((0, 0, h), (2, lo, half), (4, hi, half), (2, hi, half), (4, lo, half))):
            out += [(here[k], slot, f, rows), (there[k], slot + 1, f, rows)]
        return out

    blocks = [block(dist, s) for dist in (0, 1, 3) for s in (0, 1)]
    z, x_all = head_product(after(wt_p, c, d), early((own_p, a_p, b_p, a2_p, b2_p), there), blocks, keep=True)
    c2 = lax.ppermute(c, "y", UP_Y)
    d2 = lax.ppermute(d, "y", DOWN_Y)
    here_r = (own_r, a_r, b_r, a2_r, b2_r)
    there_r = [swap(after(arr, z, c2, d2)) for arr in here_r]
    (r,) = head_product(wt_r, early(here_r, there_r), blocks, keep=False)

    last = (c, d, c2, d2)
    last_there = [swap(arr) for arr in last]
    marks = jnp.stack((marks, a_p[half:], c[2 * quarter :], b_p[half:]))
    marks = jnp.stack((marks, jnp.stack((swap(marks[0]), there[1][half:], last_there[0][2 * quarter :], there[2][half:]))))
    marks = marks[:, :, :6].astype(F32)
    labels = jnp.stack((marks[:, :, 0] * 4096.0 + marks[:, :, 1] * 64.0 + marks[:, :, 2], marks[:, :, 3] + marks[:, :, 4] + marks[:, :, 5]), axis=2)
    labels = jnp.where(ic == 0, labels, labels[::-1])
    labels = jnp.concatenate((labels, labels), axis=1)
    labels = lax.dynamic_slice_in_dim(labels, NX - ix, NX, 1).reshape(NC * NX, 2, OWN)

    first = ((((ix * NC + ic) * NZ + iz) * NY + iy) * width).astype(I32)
    stats = row_stats(first, blocks, z, r, labels)
    late = []
    for arr, arr_there, f in zip(last, last_there, (lo + skip, hi + skip, hi + rest, lo + rest)):
        late += [(arr, 0, f, quarter), (arr_there, 1, f, quarter)]
    z, r, x_all, stats = late_product(first, labels, wt_p, wt_r, late, [block(2, s) for s in (0, 1)], z, r, x_all, stats)

    stats = all_merge(stats)
    g, far_other, near_other = grad_and_terms(first, 1 - ic, term_places(ic == 1, ix, iy), labels, stats, z, r, w_yz)
    far_mine, near_mine = own_terms(ic, term_places(ic == 0, ix, iy), g, w_yz)
    far_other = swap(far_other)
    near_other = swap(near_other)
    far = add(far_mine, far_other)
    via_up = lax.ppermute(far[:2], ALL, core_route(1, False))
    via_down = lax.ppermute(far[2:], ALL, core_route(-1, False))
    near = near_mine.astype(F32) + near_other.astype(F32)
    to_up = jnp.concatenate(((near[0, :2] + via_up.astype(F32)).astype(BF), near[0, 2:].astype(BF)), axis=0)
    to_down = jnp.concatenate((near[1, :2].astype(BF), (near[1, 2:] + via_down.astype(F32)).astype(BF)), axis=0)
    from_down = lax.ppermute(to_up, ALL, core_route(1, False))
    from_up = lax.ppermute(to_down, ALL, core_route(-1, False))
    d_policy = d_policy_of(x_all, after(g, to_up, to_down))
    from_down, from_up, d_policy = lax.optimization_barrier((from_down, from_up, d_policy))
    parts = near[2] + from_down.astype(F32) + from_up.astype(F32)

    at = jnp.where(ic == 0, iy, ix)
    total = lax.dynamic_index_in_dim(parts, at, 0, keepdims=False)
    parts = parts.astype(BF)
    for dist in (1, 3, 2):
        part = lax.dynamic_index_in_dim(parts, (at + dist) % NX, 0, keepdims=False)
        total = total + lax.ppermute(part, ALL, core_route(dist, True)).astype(F32)
    total = total.astype(BF).reshape(NZ, padded, OWN)
    got = lax.all_to_all(total, "z", split_axis=0, concat_axis=0, tiled=True)
    d_hidden = jnp.sum(got.astype(F32), axis=0)[:piece].T

    mine = lax.dynamic_index_in_dim(stats, block(0, 0), 0, keepdims=False)
    lse_z, _, entropy, kl = row_results(mine)
    return (mine[6] - lse_z[0], entropy[0], kl[0], d_hidden, d_policy)


def solution(mesh):
    fine = Mesh(mesh.devices.reshape(NX, NC, NZ, NY), ("x", "core", "z", "y"))
    dp, vocab = ("x", "core"), ("z", "y")
    everybody = dp + vocab
    in_specs = (P(dp, None), P(dp, None), P(dp), P(dp), P(None, everybody), P(None, everybody))
    out_specs = (P(dp), P(dp), P(dp), P(dp, vocab), P(None, everybody))
    return jax.shard_map(shards, mesh=fine, in_specs=in_specs, out_specs=out_specs, check_vma=False)
```

```python
import functools

import jax
import jax.numpy as jnp
from jax import lax
from jax.experimental import pallas as pl
from jax.experimental.pallas import tpu as pltpu
from jax.sharding import Mesh, PartitionSpec as P

NX, NC, NZ, NY = 4, 2, 8, 4
OWN = 128
BF, F32, I32 = jnp.bfloat16, jnp.float32, jnp.int32
LIMIT, SMALL = 24 * 1024 * 1024, 16 * 1024 * 1024
VMEM, SMEM, HBM = pltpu.VMEM, pltpu.SMEM, pltpu.HBM


def params(limit=LIMIT):
    return pltpu.CompilerParams(vmem_limit_bytes=limit)


def in_hbm(a):
    return pltpu.with_memory_space_constraint(a, HBM)


def split(n, parts):
    step = -(-n // (16 * parts)) * 16
    return [(k, min(step, n - k)) for k in range(0, n, step)]


def cost(flops, nbytes, trans=0):
    return pl.CostEstimate(flops=int(flops), bytes_accessed=int(nbytes), transcendentals=int(trans))


def lanes(s):
    return pl.ds(pl.multiple_of(s * OWN, OWN), OWN)


def prep_kernel(piece, n_out, w_hbm, *refs):
    wt_hbm, wr_hbm = refs[0], refs[1 if n_out == 2 else 0]
    wbuf, tbuf, rbuf, in_sem, t_sem, r_sem = refs[n_out:]
    n, h, _ = wbuf.shape

    def load(s):
        return [
            pltpu.make_async_copy(w_hbm.at[pl.ds(k, m), lanes(s)], wbuf.at[s, pl.ds(k, m)], in_sem.at[s, i])
            for i, (k, m) in enumerate(split(h, 4))
        ]

    def store(s):
        copies = []
        for i, (k, m) in enumerate(split(OWN, 4)):
            rows = pl.ds(pl.multiple_of(s * OWN + k, 16), m)
            copies.append(pltpu.make_async_copy(tbuf.at[s, pl.ds(k, m)], wt_hbm.at[rows], t_sem.at[s, i]))
        if n_out == 2:
            for y in range(NY):
                copies.append(pltpu.make_async_copy(rbuf.at[s, y], wr_hbm.at[y, :, :, lanes(s)], r_sem.at[s, y]))
        return copies

    for s in range(n):
        for copy in load(s):
            copy.start()

    def step(s, _):
        for copy in load(s):
            copy.wait()
        w = wbuf[s]
        tbuf[s] = w.T
        if n_out == 2:
            fill = jnp.zeros((rbuf.shape[3] - piece, OWN), w.dtype)
            for z in range(NZ):
                for y in range(NY):
                    k = (z * NY + y) * piece
                    rbuf[s, y, z] = jnp.concatenate((w[k : k + piece], fill), axis=0)
        for copy in store(s):
            copy.start()
        return 0

    lax.fori_loop(0, n, step, 0)
    for s in range(n):
        for copy in store(s):
            copy.wait()


def prep(w, padded=None):
    h, width = w.shape
    n = width // OWN
    out_shape = [HBM((width, h), BF)]
    if padded:
        out_shape.append(HBM((NY, NZ, padded, width), BF))
    return pl.pallas_call(
        functools.partial(prep_kernel, h // (NZ * NY), len(out_shape)),
        out_shape=out_shape,
        in_specs=[pl.BlockSpec(memory_space=pl.ANY)],
        out_specs=[pl.BlockSpec(memory_space=pl.ANY)] * len(out_shape),
        scratch_shapes=[
            VMEM((n, h, OWN), BF),
            VMEM((n, OWN, h), BF),
            VMEM((n if padded else 1, NY, NZ, padded or 16, OWN), BF),
            pltpu.SemaphoreType.DMA((n, 4)),
            pltpu.SemaphoreType.DMA((n, 4)),
            pltpu.SemaphoreType.DMA((n, NY)),
        ],
        compiler_params=params(SMALL),
        cost_estimate=cost(0, 6 * h * width),
    )(in_hbm(w))


TILES, WT_PARTS = 2, 4


def tile_rows(t, width):
    tile = width // TILES
    return pl.ds(pl.multiple_of(t * tile, tile), tile)


def wt_loads(t, src, dst, sem):
    tile = src.shape[0] // TILES
    part = tile // WT_PARTS
    rows = [pl.ds(pl.multiple_of(t * tile + i * part, 16), part) for i in range(WT_PARTS)]
    return [pltpu.make_async_copy(src.at[k], dst.at[k], sem.at[t, i]) for i, k in enumerate(rows)]


def head_kernel(plan, slots, n_in, n_prev, n_out, info_ref, wt_hbm, *refs):
    arrays = refs[:n_in]
    outs = refs[n_in + n_prev : n_in + n_prev + n_out]
    wt, xs, obuf, wt_sem, in_sem, out_sem, keep_sem = refs[n_in + n_prev + n_out :]
    copies = []
    for i, (at, slot, rows) in enumerate(plan):
        first = pl.multiple_of(info_ref[slots + i], 16)
        src = arrays[at].at[pl.ds(0, rows)]
        copy = pltpu.make_async_copy(src, xs.at[pl.ds(first, rows), pl.ds(slot * OWN, OWN)], in_sem.at[i])
        copy.start()
        copies.append(copy)
    for t in range(TILES):
        for copy in wt_loads(t, wt_hbm, wt, wt_sem):
            copy.start()
    for copy in copies:
        copy.wait()
    kept = []
    if n_out == 2:
        for s in range(slots):
            copy = pltpu.make_async_copy(xs.at[:, pl.ds(s * OWN, OWN)], outs[1].at[info_ref[s]], keep_sem.at[s])
            copy.start()
            kept.append(copy)
    width = wt.shape[0]

    def store(t):
        rows = tile_rows(t, width)
        return [
            pltpu.make_async_copy(obuf.at[s, rows], outs[0].at[info_ref[s], rows], out_sem.at[t, s]) for s in range(slots)
        ]

    def step(t, _):
        for copy in wt_loads(t, wt_hbm, wt, wt_sem):
            copy.wait()
        rows = tile_rows(t, width)
        acc = jnp.dot(wt[rows, :], xs[...], preferred_element_type=F32)
        for s in range(slots):
            obuf[s, rows, :] = acc[:, s * OWN : (s + 1) * OWN]
        for copy in store(t):
            copy.start()
        return 0

    lax.fori_loop(0, TILES, step, 0)
    for t in range(TILES):
        for copy in store(t):
            copy.wait()
    for copy in kept:
        copy.wait()


def head_product(wt, pieces, slot_blocks, keep, prev=()):
    width, h = wt.shape
    slots = len(slot_blocks)
    arrays = [arr for arr, _, _, _ in pieces]
    plan = [(i, slot, rows) for i, (_, slot, _, rows) in enumerate(pieces)]
    info = jnp.stack([jnp.asarray(v, I32) for v in slot_blocks] + [jnp.asarray(f, I32) for _, _, f, _ in pieces])
    out_shape = [HBM((NX * NC, width, OWN), F32)]
    if keep:
        out_shape.append(HBM((NX * NC, h, OWN), BF))
    any_spec = pl.BlockSpec(memory_space=pl.ANY)
    n_in = len(arrays)
    return pl.pallas_call(
        functools.partial(head_kernel, plan, slots, n_in, len(prev), len(out_shape)),
        out_shape=out_shape,
        in_specs=[pl.BlockSpec(memory_space=SMEM)] + [any_spec] * (1 + n_in + len(prev)),
        out_specs=[any_spec] * len(out_shape),
        scratch_shapes=[
            VMEM((width, h), BF),
            VMEM((h, slots * OWN), BF),
            VMEM((slots, width, OWN), F32),
            pltpu.SemaphoreType.DMA((TILES, WT_PARTS)),
            pltpu.SemaphoreType.DMA((len(plan),)),
            pltpu.SemaphoreType.DMA((TILES, slots)),
            pltpu.SemaphoreType.DMA((slots,)),
        ],
        input_output_aliases={2 + n_in + k: k for k in range(len(prev))},
        compiler_params=params(SMALL),
        cost_estimate=cost(2 * width * h * slots * OWN, width * h * 2 + slots * OWN * (h * 2 + width * 4)),
    )(info, in_hbm(wt), *arrays, *prev)


def stats_rows(z, r, ids, first):
    col = (lax.broadcasted_iota(I32, z.shape, 0) + first).astype(F32)
    m_z = jnp.max(z, axis=0, keepdims=True)
    m_r = jnp.max(r, axis=0, keepdims=True)
    e = jnp.exp(z - m_z)
    rows = (
        m_z,
        jnp.sum(e, axis=0, keepdims=True),
        jnp.sum(e * z, axis=0, keepdims=True),
        jnp.sum(e * r, axis=0, keepdims=True),
        m_r,
        jnp.sum(jnp.exp(r - m_r), axis=0, keepdims=True),
        jnp.sum(jnp.where(col == ids, z, 0.0), axis=0, keepdims=True),
        jnp.zeros_like(m_z),
    )
    return jnp.concatenate(rows, axis=0)


def stats_kernel(n, info_ref, lab_ref, z_hbm, r_hbm, out_ref, zb, rb, sem):
    def load(k):
        at = info_ref[k + 1]
        return (
            pltpu.make_async_copy(z_hbm.at[at], zb.at[k], sem.at[0, k]),
            pltpu.make_async_copy(r_hbm.at[at], rb.at[k], sem.at[1, k]),
        )

    for k in range(n):
        for copy in load(k):
            copy.start()

    def step(k, _):
        for copy in load(k):
            copy.wait()
        at = info_ref[k + 1]
        out_ref[at] = stats_rows(zb[k], rb[k], lab_ref[at, 0:1], info_ref[0])
        return 0

    lax.fori_loop(0, n, step, 0)


def row_stats(first, blocks, z, r, labels):
    width, n = z.shape[1], len(blocks)
    info = jnp.stack([first] + [jnp.asarray(b, I32) for b in blocks])
    return pl.pallas_call(
        functools.partial(stats_kernel, n),
        out_shape=jax.ShapeDtypeStruct((z.shape[0], 8, OWN), F32),
        in_specs=[pl.BlockSpec(memory_space=SMEM), pl.BlockSpec(memory_space=VMEM)] + [pl.BlockSpec(memory_space=pl.ANY)] * 2,
        out_specs=pl.BlockSpec(memory_space=VMEM),
        scratch_shapes=[VMEM((n, width, OWN), F32), VMEM((n, width, OWN), F32), pltpu.SemaphoreType.DMA((2, n))],
        compiler_params=params(SMALL),
        cost_estimate=cost(12 * z.size, 6 * z.size, 2 * z.size),
    )(info, labels, in_hbm(z), in_hbm(r))


def late_kernel(plan, n_in, info_ref, lab_ref, wp_hbm, wr_hbm, *refs):
    arrays = refs[:n_in]
    z_out, r_out, x_out, st_out = refs[n_in + 4 : n_in + 8]
    wts, xs, obuf, stbuf, wt_sem, in_sem, out_sem, keep_sem, st_sem = refs[n_in + 8 :]
    weights = (wp_hbm, wr_hbm)
    copies = [[], []]
    for head in range(2):
        for i, (at, slot, rows) in enumerate(plan):
            first = pl.multiple_of(info_ref[3 + i], 16)
            dst = xs.at[head, pl.ds(first, rows), pl.ds(slot * OWN, OWN)]
            copy = pltpu.make_async_copy(arrays[at].at[pl.ds(head * rows, rows)], dst, in_sem.at[head, i])
            copy.start()
            copies[head].append(copy)
        for t in range(TILES):
            for copy in wt_loads(t, weights[head], wts.at[head], wt_sem.at[head]):
                copy.start()
    width = wts.shape[1]
    done = []
    for head, out in enumerate((z_out, r_out)):
        for copy in copies[head]:
            copy.wait()
        if head == 0:
            for s in range(2):
                copy = pltpu.make_async_copy(xs.at[0, :, pl.ds(s * OWN, OWN)], x_out.at[info_ref[1 + s]], keep_sem.at[s])
                copy.start()
                done.append(copy)

        def store(t):
            rows = tile_rows(t, width)
            return [
                pltpu.make_async_copy(obuf.at[head, s, rows], out.at[info_ref[1 + s], rows], out_sem.at[head, t, s])
                for s in range(2)
            ]

        def step(t, _):
            for copy in wt_loads(t, weights[head], wts.at[head], wt_sem.at[head]):
                copy.wait()
            rows = tile_rows(t, width)
            acc = jnp.dot(wts[head, rows, :], xs[head], preferred_element_type=F32)
            for s in range(2):
                obuf[head, s, rows, :] = acc[:, s * OWN : (s + 1) * OWN]
            for copy in store(t):
                copy.start()
            return 0

        lax.fori_loop(0, TILES, step, 0)
        for t in range(TILES):
            done += store(t)
    for s in range(2):
        stbuf[s] = stats_rows(obuf[0, s], obuf[1, s], lab_ref[info_ref[1 + s], 0:1], info_ref[0])
        copy = pltpu.make_async_copy(stbuf.at[s], st_out.at[info_ref[1 + s]], st_sem.at[s])
        copy.start()
        done.append(copy)
    for copy in done:
        copy.wait()


def late_product(first, labels, wt_p, wt_r, pieces, blocks, z, r, x_all, stats):
    width, h = wt_p.shape
    plan = [(i, slot, rows) for i, (_, slot, _, rows) in enumerate(pieces)]
    info = jnp.stack([first] + [jnp.asarray(v, I32) for v in blocks] + [jnp.asarray(f, I32) for _, _, f, _ in pieces])
    n_in = len(pieces)
    hbm = pl.BlockSpec(memory_space=pl.ANY)
    prev = [in_hbm(a) for a in (z, r, x_all)] + [stats]
    return pl.pallas_call(
        functools.partial(late_kernel, plan, n_in),
        out_shape=[HBM(a.shape, a.dtype) for a in prev[:3]] + [jax.ShapeDtypeStruct(stats.shape, F32)],
        in_specs=[pl.BlockSpec(memory_space=SMEM), pl.BlockSpec(memory_space=VMEM)] + [hbm] * (2 + n_in + 4),
        out_specs=[hbm] * 4,
        scratch_shapes=[
            VMEM((2, width, h), BF),
            VMEM((2, h, 2 * OWN), BF),
            VMEM((2, 2, width, OWN), F32),
            VMEM((2, 8, OWN), F32),
            pltpu.SemaphoreType.DMA((2, TILES, WT_PARTS)),
            pltpu.SemaphoreType.DMA((2, n_in)),
            pltpu.SemaphoreType.DMA((2, TILES, 2)),
            pltpu.SemaphoreType.DMA((2,)),
            pltpu.SemaphoreType.DMA((2,)),
        ],
        input_output_aliases={4 + n_in + k: k for k in range(4)},
        compiler_params=params(SMALL),
        cost_estimate=cost(8 * width * h * OWN, 4 * width * h + 8 * OWN * (h + width)),
    )(info, labels, in_hbm(wt_p), in_hbm(wt_r), *[arr for arr, _, _, _ in pieces], *prev)


def merge_kernel(*refs):
    ins, out = refs[:-1], refs[-1]
    row = lambda ref, k: ref[:, k : k + 1]
    for top, sums in ((0, (1, 2, 3)), (4, (5,))):
        peak = functools.reduce(jnp.maximum, [row(ref, top) for ref in ins])
        scale = [jnp.exp(row(ref, top) - peak) for ref in ins]
        out[:, top : top + 1] = peak
        for k in sums:
            out[:, k : k + 1] = sum(w * row(ref, k) for w, ref in zip(scale, ins))
    for k in (6, 7):
        out[:, k : k + 1] = sum(row(ref, k) for ref in ins)


def merge(*stats):
    return pl.pallas_call(
        merge_kernel,
        out_shape=jax.ShapeDtypeStruct(stats[0].shape, F32),
        compiler_params=params(),
        cost_estimate=cost(10 * stats[0].size * len(stats), 4 * stats[0].size * (len(stats) + 1)),
    )(*stats)


def by_xor(n, k):
    return [(i, i ^ k) for i in range(n)]


def by_shift(n, k):
    return [(i, (i + k) % n) for i in range(n)]


def all_merge(stats):
    for axis, n, rounds in (
        ("core", NC, (by_xor(NC, 1),)),
        ("x", NX, (by_xor(NX, 1), by_xor(NX, 3))),
        ("y", NY, (by_xor(NY, 1), by_xor(NY, 3))),
        ("z", NZ, (by_xor(NZ, 1), by_xor(NZ, 2), [(i, ((6 if i % 2 == 0 else 8) - i) % NZ) for i in range(NZ)])),
    ):
        for pairs in rounds:
            stats = merge(stats, lax.ppermute(stats, axis, pairs))
    return stats


def row_results(st):
    lse_z = st[0:1] + jnp.log(st[1:2])
    lse_r = st[4:5] + jnp.log(st[5:6])
    entropy = lse_z - st[2:3] / st[1:2]
    kl = (st[2:3] - st[3:4]) / st[1:2] - lse_z + lse_r
    return lse_z, lse_r, entropy, kl


def grad_of(z, r, ids, adv, st, first):
    col = (lax.broadcasted_iota(I32, z.shape, 0) + first).astype(F32)
    lse_z, lse_r, entropy, kl = row_results(st)
    lp = z - lse_z
    lq = r - lse_r
    p = jnp.exp(lp)
    hot = jnp.where(col == ids, 1.0, 0.0)
    return (-adv * (hot - p) + 0.1 * p * (lp - lq - kl) + 0.05 * p * (lp + entropy)).astype(BF)


W_PARTS = 2


def w_loads(y, w_hbm, wb, sem):
    return [
        pltpu.make_async_copy(w_hbm.at[y, pl.ds(k, m)], wb.at[y, pl.ds(k, m)], sem.at[y, i])
        for i, (k, m) in enumerate(split(wb.shape[1], W_PARTS))
    ]


def term_loop(info_ref, base, load_w, wb, rows_of, far_ref, near_ref):
    def step(y, _):
        for copy in load_w(y):
            copy.wait()
        rows = jnp.concatenate([rows_of(x) for x in range(NX)], axis=1)
        acc = jnp.dot(wb[y], rows, preferred_element_type=F32).astype(BF)
        for x in range(NX):
            at = base + 2 * (y * NX + x)
            group, k = info_ref[at], info_ref[at + 1]

            @pl.when(group == 0)
            def _():
                far_ref[k] = acc[:, x * OWN : (x + 1) * OWN]

            @pl.when(group > 0)
            def _():
                near_ref[group - 1, k] = acc[:, x * OWN : (x + 1) * OWN]

        return 0

    lax.fori_loop(0, NY, step, 0)


def grad_term_kernel(info_ref, lab_ref, st_ref, z_hbm, r_hbm, w_hbm, g_hbm, far_ref, near_ref, zb, rb, wb, gb, in_sem, w_sem, g_sem):
    n = zb.shape[0]

    def load(k):
        return (
            pltpu.make_async_copy(z_hbm.at[k], zb.at[k], in_sem.at[0, k]),
            pltpu.make_async_copy(r_hbm.at[k], rb.at[k], in_sem.at[1, k]),
        )

    def load_w(y):
        return w_loads(y, w_hbm, wb, w_sem)

    def store(k):
        return pltpu.make_async_copy(gb.at[k], g_hbm.at[k], g_sem.at[k])

    for k in range(n):
        for copy in load(k):
            copy.start()

    def step(k, _):
        for copy in load(k):
            copy.wait()

        @pl.when(k < NY)
        def _():
            for copy in load_w(k):
                copy.start()

        gb[k] = grad_of(zb[k], rb[k], lab_ref[k, 0:1], lab_ref[k, 1:2], st_ref[k], info_ref[0])
        store(k).start()
        return 0

    lax.fori_loop(0, n, step, 0)
    term_loop(info_ref, 2, load_w, wb, lambda x: gb[info_ref[1] * NX + x], far_ref, near_ref)
    for k in range(n):
        store(k).wait()


def own_term_kernel(info_ref, w_hbm, g_hbm, far_ref, near_ref, wb, gb, w_sem, g_sem):
    def load_w(y):
        return w_loads(y, w_hbm, wb, w_sem)

    def load_g(x):
        return pltpu.make_async_copy(g_hbm.at[info_ref[0] * NX + x], gb.at[x], g_sem.at[x])

    for x in range(NX):
        load_g(x).start()
    for y in range(NY):
        for copy in load_w(y):
            copy.start()
    for x in range(NX):
        load_g(x).wait()
    term_loop(info_ref, 1, load_w, wb, lambda x: gb[x], far_ref, near_ref)


def term_places(to_x, ix, iy):
    out = []
    for y in range(NY):
        for x in range(NX):
            distance = jnp.where(to_x, x - ix, y - iy) % NX
            group = jnp.where(distance == 0, 3, jnp.where(distance == 1, 1, jnp.where(distance == 2, 0, 2)))
            out += [group, jnp.where(to_x, y, x)]
    return out


def pack(values):
    return jnp.stack([jnp.asarray(v, I32) for v in values])


def term_shapes(m):
    return [jax.ShapeDtypeStruct((NX, m, OWN), BF), jax.ShapeDtypeStruct((NX - 1, NX, m, OWN), BF)]


def grad_and_terms(first, core, places, labels, stats, z, r, w):
    n, width, _ = z.shape
    m = w.shape[1]
    hbm, vmem = pl.BlockSpec(memory_space=pl.ANY), pl.BlockSpec(memory_space=VMEM)
    return pl.pallas_call(
        grad_term_kernel,
        out_shape=[HBM(z.shape, BF)] + term_shapes(m),
        in_specs=[pl.BlockSpec(memory_space=SMEM), vmem, vmem, hbm, hbm, hbm],
        out_specs=[hbm, vmem, vmem],
        scratch_shapes=[
            VMEM(z.shape, F32),
            VMEM(z.shape, F32),
            VMEM(w.shape, BF),
            VMEM(z.shape, BF),
            pltpu.SemaphoreType.DMA((2, n)),
            pltpu.SemaphoreType.DMA((NY, W_PARTS)),
            pltpu.SemaphoreType.DMA((n,)),
        ],
        compiler_params=params(),
        cost_estimate=cost(2 * w.size * NX * OWN + 16 * z.size, 10 * z.size + 2 * w.size + 8 * m * NX * OWN, z.size),
    )(pack([first, core] + places), labels, stats, in_hbm(z), in_hbm(r), in_hbm(w))


def own_terms(core, places, g, w):
    m, width = w.shape[1:]
    hbm, vmem = pl.BlockSpec(memory_space=pl.ANY), pl.BlockSpec(memory_space=VMEM)
    return pl.pallas_call(
        own_term_kernel,
        out_shape=term_shapes(m),
        in_specs=[pl.BlockSpec(memory_space=SMEM), hbm, hbm],
        out_specs=[vmem, vmem],
        scratch_shapes=[
            VMEM(w.shape, BF),
            VMEM((NX, width, OWN), BF),
            pltpu.SemaphoreType.DMA((NY, W_PARTS)),
            pltpu.SemaphoreType.DMA((NX,)),
        ],
        compiler_params=params(),
        cost_estimate=cost(2 * w.size * NX * OWN, 2 * w.size + g.size + 8 * m * NX * OWN),
    )(pack([core] + places), in_hbm(w), in_hbm(g))


def d_policy_kernel(x_hbm, g_hbm, out_hbm, xb, gb, ob, x_sem, g_sem, o_sem):
    tiles, _, m, _ = xb.shape

    def rows(t):
        return pl.ds(pl.multiple_of(t * m, 16), m)

    n = gb.shape[0]

    def load(t):
        return pltpu.make_async_copy(x_hbm.at[:, rows(t)], xb.at[t], x_sem.at[t])

    def store(t):
        return pltpu.make_async_copy(ob.at[t], out_hbm.at[rows(t)], o_sem.at[t])

    load_g = [pltpu.make_async_copy(g_hbm.at[b], gb.at[b], g_sem.at[b]) for b in range(n)]
    for copy in load_g:
        copy.start()
    for t in range(tiles):
        load(t).start()
    for copy in load_g:
        copy.wait()

    def step(t, _):
        load(t).wait()
        acc = 0.0
        for j in range(0, NX * NC, 2):
            lhs = jnp.concatenate((xb[t, j], xb[t, j + 1]), axis=1)
            rhs = jnp.concatenate((gb[j], gb[j + 1]), axis=1)
            acc = acc + lax.dot_general(lhs, rhs, (((1,), (1,)), ((), ())), preferred_element_type=F32)
        ob[t] = acc.astype(BF)
        store(t).start()
        return 0

    lax.fori_loop(0, tiles, step, 0)
    for t in range(tiles):
        store(t).wait()


def d_policy_of(x, g):
    n, h, _ = x.shape
    width = g.shape[1]
    tiles = 6
    m = h // tiles
    hbm = pl.BlockSpec(memory_space=pl.ANY)
    return pl.pallas_call(
        d_policy_kernel,
        out_shape=jax.ShapeDtypeStruct((h, width), BF),
        in_specs=[hbm, hbm],
        out_specs=hbm,
        scratch_shapes=[
            VMEM((tiles, n, m, OWN), BF),
            VMEM(g.shape, BF),
            VMEM((tiles, m, width), BF),
            pltpu.SemaphoreType.DMA((tiles,)),
            pltpu.SemaphoreType.DMA((n,)),
            pltpu.SemaphoreType.DMA((tiles,)),
        ],
        compiler_params=params(),
        cost_estimate=cost(2 * h * width * n * OWN, 2 * (x.size + g.size + h * width)),
    )(in_hbm(x), in_hbm(g))


UP_X, DOWN_X = by_shift(NX, 1), by_shift(NX, NX - 1)
UP_Y, DOWN_Y = by_shift(NY, 1), by_shift(NY, NY - 1)
ALL = ("x", "core", "z", "y")


def swap(a):
    return lax.ppermute(a, "core", by_xor(NC, 1))


def cut(a, first, n):
    return lax.dynamic_slice_in_dim(a, first, n, 0)


def core_route(d, second):
    pairs = []
    for x in range(NX):
        for c in range(NC):
            for z in range(NZ):
                for y in range(NY):
                    along_x = (c == 0) != second
                    x2, y2 = ((x + d) % NX, y) if along_x else (x, (y + d) % NY)
                    pairs.append((((x * NC + c) * NZ + z) * NY + y, ((x2 * NC + c) * NZ + z) * NY + y2))
    return pairs


def label_rows(ids, adv):
    top = lax.reduce_precision(adv, 8, 7)
    middle = lax.reduce_precision(adv - top, 8, 7)
    parts = [(ids >> 12).astype(F32), ((ids >> 6) & 63).astype(F32), (ids & 63).astype(F32), top, middle, adv - top - middle]
    return jnp.pad(jnp.stack(parts).astype(BF), ((0, 10), (0, 0)))


def add(a, b):
    return (a.astype(F32) + b.astype(F32)).astype(BF)


def after(value, *first):
    return lax.optimization_barrier((value, *first))[0]


def shards(hidden, ref_hidden, sampled, advantage, policy_head, ref_head):
    ix, ic, iz, iy = (lax.axis_index(a) for a in ALL)
    h, width = policy_head.shape
    half, quarter = h // 2, h // 4
    odd = iy % 2
    lo, hi, skip = odd * half, (1 - odd) * half, odd * quarter
    piece = h // (NZ * NY)
    padded = -(-piece // 16) * 16

    def block(d, other):
        return (ic ^ other) * NX + (ix + d) % NX

    own_p, own_r = hidden.T, ref_hidden.T
    marks = label_rows(sampled, advantage)
    a_p = lax.ppermute(jnp.concatenate((cut(own_p, lo, half), marks), axis=0), "x", DOWN_X)
    b_p = lax.ppermute(jnp.concatenate((cut(own_p, hi, half), marks), axis=0), "x", UP_X)
    a_r = lax.ppermute(cut(own_r, lo, half), "x", DOWN_X)
    b_r = lax.ppermute(cut(own_r, hi, half), "x", UP_X)

    wt_p, w_yz = prep(policy_head, padded)
    w_yz = w_yz.reshape(NY, NZ * padded, width)
    (wt_r,) = prep(after(ref_head, wt_p))
    a_p, b_p, wt_p, wt_r = lax.optimization_barrier((a_p, b_p, wt_p, wt_r))
    a2_p = lax.ppermute(a_p, "y", UP_Y)
    b2_p = lax.ppermute(b_p, "y", DOWN_Y)
    there = [swap(arr) for arr in (own_p, a_p, b_p)]
    a_r, b_r, *there = lax.optimization_barrier((a_r, b_r, *there))
    c = jnp.concatenate((cut(a_p, skip, quarter), cut(a_r, skip, quarter), a_p[half:]), axis=0)
    d = jnp.concatenate((cut(b_p, skip, quarter), cut(b_r, skip, quarter), b_p[half:]), axis=0)
    there += [swap(after(arr, c, d)) for arr in (a2_p, b2_p)]
    c = lax.ppermute(c, "x", DOWN_X)
    d = lax.ppermute(d, "x", UP_X)
    a2_r = lax.ppermute(a_r, "y", UP_Y)
    b2_r = lax.ppermute(b_r, "y", DOWN_Y)
    rest = quarter - skip

    def early(here, there):
        out = []
        for k, (slot, f, rows) in enumerate(((0, 0, h), (2, lo, half), (4, hi, half), (2, hi, half), (4, lo, half))):
            out += [(here[k], slot, f, rows), (there[k], slot + 1, f, rows)]
        return out

    blocks = [block(dist, s) for dist in (0, 1, 3) for s in (0, 1)]
    z, x_all = head_product(after(wt_p, c, d), early((own_p, a_p, b_p, a2_p, b2_p), there), blocks, keep=True)
    c2 = lax.ppermute(c, "y", UP_Y)
    d2 = lax.ppermute(d, "y", DOWN_Y)
    here_r = (own_r, a_r, b_r, a2_r, b2_r)
    there_r = [swap(after(arr, z, c2, d2)) for arr in here_r]
    (r,) = head_product(wt_r, early(here_r, there_r), blocks, keep=False)

    last = (c, d, c2, d2)
    last_there = [swap(arr) for arr in last]
    marks = jnp.stack((marks, a_p[half:], c[2 * quarter :], b_p[half:]))
    marks = jnp.stack((marks, jnp.stack((swap(marks[0]), there[1][half:], last_there[0][2 * quarter :], there[2][half:]))))
    marks = marks[:, :, :6].astype(F32)
    labels = jnp.stack((marks[:, :, 0] * 4096.0 + marks[:, :, 1] * 64.0 + marks[:, :, 2], marks[:, :, 3] + marks[:, :, 4] + marks[:, :, 5]), axis=2)
    labels = jnp.where(ic == 0, labels, labels[::-1])
    labels = jnp.concatenate((labels, labels), axis=1)
    labels = lax.dynamic_slice_in_dim(labels, NX - ix, NX, 1).reshape(NC * NX, 2, OWN)

    first = ((((ix * NC + ic) * NZ + iz) * NY + iy) * width).astype(I32)
    stats = row_stats(first, blocks, z, r, labels)
    late = []
    for arr, arr_there, f in zip(last, last_there, (lo + skip, hi + skip, hi + rest, lo + rest)):
        late += [(arr, 0, f, quarter), (arr_there, 1, f, quarter)]
    z, r, x_all, stats = late_product(first, labels, wt_p, wt_r, late, [block(2, s) for s in (0, 1)], z, r, x_all, stats)

    stats = all_merge(stats)
    g, far_other, near_other = grad_and_terms(first, 1 - ic, term_places(ic == 1, ix, iy), labels, stats, z, r, w_yz)
    far_mine, near_mine = own_terms(ic, term_places(ic == 0, ix, iy), g, w_yz)
    far_other = swap(far_other)
    near_other = swap(near_other)
    far = add(far_mine, far_other)
    via_up = lax.ppermute(far[:2], ALL, core_route(1, False))
    via_down = lax.ppermute(far[2:], ALL, core_route(-1, False))
    near = near_mine.astype(F32) + near_other.astype(F32)
    to_up = jnp.concatenate(((near[0, :2] + via_up.astype(F32)).astype(BF), near[0, 2:].astype(BF)), axis=0)
    to_down = jnp.concatenate((near[1, :2].astype(BF), (near[1, 2:] + via_down.astype(F32)).astype(BF)), axis=0)
    from_down = lax.ppermute(to_up, ALL, core_route(1, False))
    from_up = lax.ppermute(to_down, ALL, core_route(-1, False))
    d_policy = d_policy_of(x_all, after(g, to_up, to_down))
    from_down, from_up, d_policy = lax.optimization_barrier((from_down, from_up, d_policy))
    parts = near[2] + from_down.astype(F32) + from_up.astype(F32)

    at = jnp.where(ic == 0, iy, ix)
    total = lax.dynamic_index_in_dim(parts, at, 0, keepdims=False)
    parts = parts.astype(BF)
    for dist in (1, 3, 2):
        part = lax.dynamic_index_in_dim(parts, (at + dist) % NX, 0, keepdims=False)
        total = total + lax.ppermute(part, ALL, core_route(dist, True)).astype(F32)
    total = total.astype(BF).reshape(NZ, padded, OWN)
    got = lax.all_to_all(total, "z", split_axis=0, concat_axis=0, tiled=True)
    d_hidden = jnp.sum(got.astype(F32), axis=0)[:piece].T

    mine = lax.dynamic_index_in_dim(stats, block(0, 0), 0, keepdims=False)
    lse_z, _, entropy, kl = row_results(mine)
    return (mine[6] - lse_z[0], entropy[0], kl[0], d_hidden, d_policy)


def solution(mesh):
    fine = Mesh(mesh.devices.reshape(NX, NC, NZ, NY), ("x", "core", "z", "y"))
    dp, vocab = ("x", "core"), ("z", "y")
    everybody = dp + vocab
    in_specs = (P(dp, None), P(dp, None), P(dp), P(dp), P(None, everybody), P(None, everybody))
    out_specs = (P(dp), P(dp), P(dp), P(dp, vocab), P(None, everybody))
    return jax.shard_map(shards, mesh=fine, in_specs=in_specs, out_specs=out_specs, check_vma=False)
```

```python
import functools

import jax
import jax.numpy as jnp
from jax import lax
from jax.experimental import pallas as pl
from jax.experimental.pallas import tpu as pltpu
from jax.sharding import Mesh, PartitionSpec as P

NX, NC, NZ, NY = 4, 2, 8, 4
OWN = 128
BF, F32, I32 = jnp.bfloat16, jnp.float32, jnp.int32
LIMIT, SMALL = 24 * 1024 * 1024, 16 * 1024 * 1024
VMEM, SMEM, HBM = pltpu.VMEM, pltpu.SMEM, pltpu.HBM


def params(limit=LIMIT):
    return pltpu.CompilerParams(vmem_limit_bytes=limit)


def in_hbm(a):
    return pltpu.with_memory_space_constraint(a, HBM)


def split(n, parts):
    step = -(-n // (16 * parts)) * 16
    return [(k, min(step, n - k)) for k in range(0, n, step)]


def cost(flops, nbytes, trans=0):
    return pl.CostEstimate(flops=int(flops), bytes_accessed=int(nbytes), transcendentals=int(trans))


def lanes(s):
    return pl.ds(pl.multiple_of(s * OWN, OWN), OWN)


def prep_kernel(piece, n_out, w_hbm, *refs):
    wt_hbm, wr_hbm = refs[0], refs[1 if n_out == 2 else 0]
    wbuf, tbuf, rbuf, in_sem, t_sem, r_sem = refs[n_out:]
    n, h, _ = wbuf.shape

    def load(s):
        return [
            pltpu.make_async_copy(w_hbm.at[pl.ds(k, m), lanes(s)], wbuf.at[s, pl.ds(k, m)], in_sem.at[s, i])
            for i, (k, m) in enumerate(split(h, 4))
        ]

    def store(s):
        copies = []
        for i, (k, m) in enumerate(split(OWN, 4)):
            rows = pl.ds(pl.multiple_of(s * OWN + k, 16), m)
            copies.append(pltpu.make_async_copy(tbuf.at[s, pl.ds(k, m)], wt_hbm.at[rows], t_sem.at[s, i]))
        if n_out == 2:
            for y in range(NY):
                copies.append(pltpu.make_async_copy(rbuf.at[s, y], wr_hbm.at[y, :, :, lanes(s)], r_sem.at[s, y]))
        return copies

    for s in range(n):
        for copy in load(s):
            copy.start()

    def step(s, _):
        for copy in load(s):
            copy.wait()
        w = wbuf[s]
        tbuf[s] = w.T
        if n_out == 2:
            fill = jnp.zeros((rbuf.shape[3] - piece, OWN), w.dtype)
            for z in range(NZ):
                for y in range(NY):
                    k = (z * NY + y) * piece
                    rbuf[s, y, z] = jnp.concatenate((w[k : k + piece], fill), axis=0)
        for copy in store(s):
            copy.start()
        return 0

    lax.fori_loop(0, n, step, 0)
    for s in range(n):
        for copy in store(s):
            copy.wait()


def prep(w, padded=None):
    h, width = w.shape
    n = width // OWN
    out_shape = [HBM((width, h), BF)]
    if padded:
        out_shape.append(HBM((NY, NZ, padded, width), BF))
    return pl.pallas_call(
        functools.partial(prep_kernel, h // (NZ * NY), len(out_shape)),
        out_shape=out_shape,
        in_specs=[pl.BlockSpec(memory_space=pl.ANY)],
        out_specs=[pl.BlockSpec(memory_space=pl.ANY)] * len(out_shape),
        scratch_shapes=[
            VMEM((n, h, OWN), BF),
            VMEM((n, OWN, h), BF),
            VMEM((n if padded else 1, NY, NZ, padded or 16, OWN), BF),
            pltpu.SemaphoreType.DMA((n, 4)),
            pltpu.SemaphoreType.DMA((n, 4)),
            pltpu.SemaphoreType.DMA((n, NY)),
        ],
        compiler_params=params(SMALL),
        cost_estimate=cost(0, 6 * h * width),
    )(in_hbm(w))


TILES, WT_PARTS = 2, 4


def tile_rows(t, width):
    tile = width // TILES
    return pl.ds(pl.multiple_of(t * tile, tile), tile)


def wt_loads(t, src, dst, sem):
    tile = src.shape[0] // TILES
    part = tile // WT_PARTS
    rows = [pl.ds(pl.multiple_of(t * tile + i * part, 16), part) for i in range(WT_PARTS)]
    return [pltpu.make_async_copy(src.at[k], dst.at[k], sem.at[t, i]) for i, k in enumerate(rows)]


def head_kernel(plan, slots, n_in, n_prev, n_out, info_ref, wt_hbm, *refs):
    arrays = refs[:n_in]
    outs = refs[n_in + n_prev : n_in + n_prev + n_out]
    wt, xs, obuf, wt_sem, in_sem, out_sem, keep_sem = refs[n_in + n_prev + n_out :]
    copies = []
    for i, (at, slot, rows) in enumerate(plan):
        first = pl.multiple_of(info_ref[slots + i], 16)
        src = arrays[at].at[pl.ds(0, rows)]
        copy = pltpu.make_async_copy(src, xs.at[pl.ds(first, rows), pl.ds(slot * OWN, OWN)], in_sem.at[i])
        copy.start()
        copies.append(copy)
    for t in range(TILES):
        for copy in wt_loads(t, wt_hbm, wt, wt_sem):
            copy.start()
    for copy in copies:
        copy.wait()
    kept = []
    if n_out == 2:
        for s in range(slots):
            copy = pltpu.make_async_copy(xs.at[:, pl.ds(s * OWN, OWN)], outs[1].at[info_ref[s]], keep_sem.at[s])
            copy.start()
            kept.append(copy)
    width = wt.shape[0]

    def store(t):
        rows = tile_rows(t, width)
        return [
            pltpu.make_async_copy(obuf.at[s, rows], outs[0].at[info_ref[s], rows], out_sem.at[t, s]) for s in range(slots)
        ]

    def step(t, _):
        for copy in wt_loads(t, wt_hbm, wt, wt_sem):
            copy.wait()
        rows = tile_rows(t, width)
        acc = jnp.dot(wt[rows, :], xs[...], preferred_element_type=F32)
        for s in range(slots):
            obuf[s, rows, :] = acc[:, s * OWN : (s + 1) * OWN]
        for copy in store(t):
            copy.start()
        return 0

    lax.fori_loop(0, TILES, step, 0)
    for t in range(TILES):
        for copy in store(t):
            copy.wait()
    for copy in kept:
        copy.wait()


def head_product(wt, pieces, slot_blocks, keep, prev=()):
    width, h = wt.shape
    slots = len(slot_blocks)
    arrays = [arr for arr, _, _, _ in pieces]
    plan = [(i, slot, rows) for i, (_, slot, _, rows) in enumerate(pieces)]
    info = jnp.stack([jnp.asarray(v, I32) for v in slot_blocks] + [jnp.asarray(f, I32) for _, _, f, _ in pieces])
    out_shape = [HBM((NX * NC, width, OWN), F32)]
    if keep:
        out_shape.append(HBM((NX * NC, h, OWN), BF))
    any_spec = pl.BlockSpec(memory_space=pl.ANY)
    n_in = len(arrays)
    return pl.pallas_call(
        functools.partial(head_kernel, plan, slots, n_in, len(prev), len(out_shape)),
        out_shape=out_shape,
        in_specs=[pl.BlockSpec(memory_space=SMEM)] + [any_spec] * (1 + n_in + len(prev)),
        out_specs=[any_spec] * len(out_shape),
        scratch_shapes=[
            VMEM((width, h), BF),
            VMEM((h, slots * OWN), BF),
            VMEM((slots, width, OWN), F32),
            pltpu.SemaphoreType.DMA((TILES, WT_PARTS)),
            pltpu.SemaphoreType.DMA((len(plan),)),
            pltpu.SemaphoreType.DMA((TILES, slots)),
            pltpu.SemaphoreType.DMA((slots,)),
        ],
        input_output_aliases={2 + n_in + k: k for k in range(len(prev))},
        compiler_params=params(SMALL),
        cost_estimate=cost(2 * width * h * slots * OWN, width * h * 2 + slots * OWN * (h * 2 + width * 4)),
    )(info, in_hbm(wt), *arrays, *prev)


def stats_rows(z, r, ids, first):
    col = (lax.broadcasted_iota(I32, z.shape, 0) + first).astype(F32)
    m_z = jnp.max(z, axis=0, keepdims=True)
    m_r = jnp.max(r, axis=0, keepdims=True)
    e = jnp.exp(z - m_z)
    rows = (
        m_z,
        jnp.sum(e, axis=0, keepdims=True),
        jnp.sum(e * z, axis=0, keepdims=True),
        jnp.sum(e * r, axis=0, keepdims=True),
        m_r,
        jnp.sum(jnp.exp(r - m_r), axis=0, keepdims=True),
        jnp.sum(jnp.where(col == ids, z, 0.0), axis=0, keepdims=True),
        jnp.zeros_like(m_z),
    )
    return jnp.concatenate(rows, axis=0)


def stats_kernel(n, info_ref, lab_ref, z_hbm, r_hbm, out_ref, zb, rb, sem):
    def load(k):
        at = info_ref[k + 1]
        return (
            pltpu.make_async_copy(z_hbm.at[at], zb.at[k], sem.at[0, k]),
            pltpu.make_async_copy(r_hbm.at[at], rb.at[k], sem.at[1, k]),
        )

    for k in range(n):
        for copy in load(k):
            copy.start()

    def step(k, _):
        for copy in load(k):
            copy.wait()
        at = info_ref[k + 1]
        out_ref[at] = stats_rows(zb[k], rb[k], lab_ref[at, 0:1], info_ref[0])
        return 0

    lax.fori_loop(0, n, step, 0)


def row_stats(first, blocks, z, r, labels):
    width, n = z.shape[1], len(blocks)
    info = jnp.stack([first] + [jnp.asarray(b, I32) for b in blocks])
    return pl.pallas_call(
        functools.partial(stats_kernel, n),
        out_shape=jax.ShapeDtypeStruct((z.shape[0], 8, OWN), F32),
        in_specs=[pl.BlockSpec(memory_space=SMEM), pl.BlockSpec(memory_space=VMEM)] + [pl.BlockSpec(memory_space=pl.ANY)] * 2,
        out_specs=pl.BlockSpec(memory_space=VMEM),
        scratch_shapes=[VMEM((n, width, OWN), F32), VMEM((n, width, OWN), F32), pltpu.SemaphoreType.DMA((2, n))],
        compiler_params=params(SMALL),
        cost_estimate=cost(12 * z.size, 6 * z.size, 2 * z.size),
    )(info, labels, in_hbm(z), in_hbm(r))


def late_kernel(plan, n_in, info_ref, lab_ref, wp_hbm, wr_hbm, *refs):
    arrays = refs[:n_in]
    z_out, r_out, x_out, st_out = refs[n_in + 4 : n_in + 8]
    wts, xs, obuf, stbuf, wt_sem, in_sem, out_sem, keep_sem, st_sem = refs[n_in + 8 :]
    weights = (wp_hbm, wr_hbm)
    copies = [[], []]
    for head in range(2):
        for i, (at, slot, rows) in enumerate(plan):
            first = pl.multiple_of(info_ref[3 + i], 16)
            dst = xs.at[head, pl.ds(first, rows), pl.ds(slot * OWN, OWN)]
            copy = pltpu.make_async_copy(arrays[at].at[pl.ds(head * rows, rows)], dst, in_sem.at[head, i])
            copy.start()
            copies[head].append(copy)
        for t in range(TILES):
            for copy in wt_loads(t, weights[head], wts.at[head], wt_sem.at[head]):
                copy.start()
    width = wts.shape[1]
    done = []
    for head, out in enumerate((z_out, r_out)):
        for copy in copies[head]:
            copy.wait()
        if head == 0:
            for s in range(2):
                copy = pltpu.make_async_copy(xs.at[0, :, pl.ds(s * OWN, OWN)], x_out.at[info_ref[1 + s]], keep_sem.at[s])
                copy.start()
                done.append(copy)

        def store(t):
            rows = tile_rows(t, width)
            return [
                pltpu.make_async_copy(obuf.at[head, s, rows], out.at[info_ref[1 + s], rows], out_sem.at[head, t, s])
                for s in range(2)
            ]

        def step(t, _):
            for copy in wt_loads(t, weights[head], wts.at[head], wt_sem.at[head]):
                copy.wait()
            rows = tile_rows(t, width)
            acc = jnp.dot(wts[head, rows, :], xs[head], preferred_element_type=F32)
            for s in range(2):
                obuf[head, s, rows, :] = acc[:, s * OWN : (s + 1) * OWN]
            for copy in store(t):
                copy.start()
            return 0

        lax.fori_loop(0, TILES, step, 0)
        for t in range(TILES):
            done += store(t)
    for s in range(2):
        stbuf[s] = stats_rows(obuf[0, s], obuf[1, s], lab_ref[info_ref[1 + s], 0:1], info_ref[0])
        copy = pltpu.make_async_copy(stbuf.at[s], st_out.at[info_ref[1 + s]], st_sem.at[s])
        copy.start()
        done.append(copy)
    for copy in done:
        copy.wait()


def late_product(first, labels, wt_p, wt_r, pieces, blocks, z, r, x_all, stats):
    width, h = wt_p.shape
    plan = [(i, slot, rows) for i, (_, slot, _, rows) in enumerate(pieces)]
    info = jnp.stack([first] + [jnp.asarray(v, I32) for v in blocks] + [jnp.asarray(f, I32) for _, _, f, _ in pieces])
    n_in = len(pieces)
    hbm = pl.BlockSpec(memory_space=pl.ANY)
    prev = [in_hbm(a) for a in (z, r, x_all)] + [stats]
    return pl.pallas_call(
        functools.partial(late_kernel, plan, n_in),
        out_shape=[HBM(a.shape, a.dtype) for a in prev[:3]] + [jax.ShapeDtypeStruct(stats.shape, F32)],
        in_specs=[pl.BlockSpec(memory_space=SMEM), pl.BlockSpec(memory_space=VMEM)] + [hbm] * (2 + n_in + 4),
        out_specs=[hbm] * 4,
        scratch_shapes=[
            VMEM((2, width, h), BF),
            VMEM((2, h, 2 * OWN), BF),
            VMEM((2, 2, width, OWN), F32),
            VMEM((2, 8, OWN), F32),
            pltpu.SemaphoreType.DMA((2, TILES, WT_PARTS)),
            pltpu.SemaphoreType.DMA((2, n_in)),
            pltpu.SemaphoreType.DMA((2, TILES, 2)),
            pltpu.SemaphoreType.DMA((2,)),
            pltpu.SemaphoreType.DMA((2,)),
        ],
        input_output_aliases={4 + n_in + k: k for k in range(4)},
        compiler_params=params(SMALL),
        cost_estimate=cost(8 * width * h * OWN, 4 * width * h + 8 * OWN * (h + width)),
    )(info, labels, in_hbm(wt_p), in_hbm(wt_r), *[arr for arr, _, _, _ in pieces], *prev)


def merge_kernel(*refs):
    ins, out = refs[:-1], refs[-1]
    row = lambda ref, k: ref[:, k : k + 1]
    for top, sums in ((0, (1, 2, 3)), (4, (5,))):
        peak = functools.reduce(jnp.maximum, [row(ref, top) for ref in ins])
        scale = [jnp.exp(row(ref, top) - peak) for ref in ins]
        out[:, top : top + 1] = peak
        for k in sums:
            out[:, k : k + 1] = sum(w * row(ref, k) for w, ref in zip(scale, ins))
    for k in (6, 7):
        out[:, k : k + 1] = sum(row(ref, k) for ref in ins)


def merge(*stats):
    return pl.pallas_call(
        merge_kernel,
        out_shape=jax.ShapeDtypeStruct(stats[0].shape, F32),
        compiler_params=params(),
        cost_estimate=cost(10 * stats[0].size * len(stats), 4 * stats[0].size * (len(stats) + 1)),
    )(*stats)


def by_xor(n, k):
    return [(i, i ^ k) for i in range(n)]


def by_shift(n, k):
    return [(i, (i + k) % n) for i in range(n)]


def all_merge(stats):
    for axis, n, rounds in (
        ("core", NC, (by_xor(NC, 1),)),
        ("x", NX, (by_xor(NX, 1), by_xor(NX, 3))),
        ("y", NY, (by_xor(NY, 1), by_xor(NY, 3))),
        ("z", NZ, (by_xor(NZ, 1), by_xor(NZ, 2), [(i, ((6 if i % 2 == 0 else 8) - i) % NZ) for i in range(NZ)])),
    ):
        for pairs in rounds:
            stats = merge(stats, lax.ppermute(stats, axis, pairs))
    return stats


def row_results(st):
    lse_z = st[0:1] + jnp.log(st[1:2])
    lse_r = st[4:5] + jnp.log(st[5:6])
    entropy = lse_z - st[2:3] / st[1:2]
    kl = (st[2:3] - st[3:4]) / st[1:2] - lse_z + lse_r
    return lse_z, lse_r, entropy, kl


def grad_of(z, r, ids, adv, st, first):
    col = (lax.broadcasted_iota(I32, z.shape, 0) + first).astype(F32)
    lse_z, lse_r, entropy, kl = row_results(st)
    lp = z - lse_z
    lq = r - lse_r
    p = jnp.exp(lp)
    hot = jnp.where(col == ids, 1.0, 0.0)
    return (-adv * (hot - p) + 0.1 * p * (lp - lq - kl) + 0.05 * p * (lp + entropy)).astype(BF)


W_PARTS = 2


def w_loads(y, w_hbm, wb, sem):
    return [
        pltpu.make_async_copy(w_hbm.at[y, pl.ds(k, m)], wb.at[y, pl.ds(k, m)], sem.at[y, i])
        for i, (k, m) in enumerate(split(wb.shape[1], W_PARTS))
    ]


def term_loop(info_ref, base, load_w, wb, rows_of, far_ref, near_ref):
    def step(y, _):
        for copy in load_w(y):
            copy.wait()
        rows = jnp.concatenate([rows_of(x) for x in range(NX)], axis=1)
        acc = jnp.dot(wb[y], rows, preferred_element_type=F32).astype(BF)
        for x in range(NX):
            at = base + 2 * (y * NX + x)
            group, k = info_ref[at], info_ref[at + 1]

            @pl.when(group == 0)
            def _():
                far_ref[k] = acc[:, x * OWN : (x + 1) * OWN]

            @pl.when(group > 0)
            def _():
                near_ref[group - 1, k] = acc[:, x * OWN : (x + 1) * OWN]

        return 0

    lax.fori_loop(0, NY, step, 0)


def grad_term_kernel(info_ref, lab_ref, st_ref, z_hbm, r_hbm, w_hbm, g_hbm, far_ref, near_ref, zb, rb, wb, gb, in_sem, w_sem, g_sem):
    n = zb.shape[0]

    def load(k):
        return (
            pltpu.make_async_copy(z_hbm.at[k], zb.at[k], in_sem.at[0, k]),
            pltpu.make_async_copy(r_hbm.at[k], rb.at[k], in_sem.at[1, k]),
        )

    def load_w(y):
        return w_loads(y, w_hbm, wb, w_sem)

    def store(k):
        return pltpu.make_async_copy(gb.at[k], g_hbm.at[k], g_sem.at[k])

    for k in range(n):
        for copy in load(k):
            copy.start()

    def step(k, _):
        for copy in load(k):
            copy.wait()

        @pl.when(k < NY)
        def _():
            for copy in load_w(k):
                copy.start()

        gb[k] = grad_of(zb[k], rb[k], lab_ref[k, 0:1], lab_ref[k, 1:2], st_ref[k], info_ref[0])
        store(k).start()
        return 0

    lax.fori_loop(0, n, step, 0)
    term_loop(info_ref, 2, load_w, wb, lambda x: gb[info_ref[1] * NX + x], far_ref, near_ref)
    for k in range(n):
        store(k).wait()


def own_term_kernel(info_ref, w_hbm, g_hbm, far_ref, near_ref, wb, gb, w_sem, g_sem):
    def load_w(y):
        return w_loads(y, w_hbm, wb, w_sem)

    def load_g(x):
        return pltpu.make_async_copy(g_hbm.at[info_ref[0] * NX + x], gb.at[x], g_sem.at[x])

    for x in range(NX):
        load_g(x).start()
    for y in range(NY):
        for copy in load_w(y):
            copy.start()
    for x in range(NX):
        load_g(x).wait()
    term_loop(info_ref, 1, load_w, wb, lambda x: gb[x], far_ref, near_ref)


def term_places(to_x, ix, iy):
    out = []
    for y in range(NY):
        for x in range(NX):
            distance = jnp.where(to_x, x - ix, y - iy) % NX
            group = jnp.where(distance == 0, 3, jnp.where(distance == 1, 1, jnp.where(distance == 2, 0, 2)))
            out += [group, jnp.where(to_x, y, x)]
    return out


def pack(values):
    return jnp.stack([jnp.asarray(v, I32) for v in values])


def term_shapes(m):
    return [jax.ShapeDtypeStruct((NX, m, OWN), BF), jax.ShapeDtypeStruct((NX - 1, NX, m, OWN), BF)]


def grad_and_terms(first, core, places, labels, stats, z, r, w):
    n, width, _ = z.shape
    m = w.shape[1]
    hbm, vmem = pl.BlockSpec(memory_space=pl.ANY), pl.BlockSpec(memory_space=VMEM)
    return pl.pallas_call(
        grad_term_kernel,
        out_shape=[HBM(z.shape, BF)] + term_shapes(m),
        in_specs=[pl.BlockSpec(memory_space=SMEM), vmem, vmem, hbm, hbm, hbm],
        out_specs=[hbm, vmem, vmem],
        scratch_shapes=[
            VMEM(z.shape, F32),
            VMEM(z.shape, F32),
            VMEM(w.shape, BF),
            VMEM(z.shape, BF),
            pltpu.SemaphoreType.DMA((2, n)),
            pltpu.SemaphoreType.DMA((NY, W_PARTS)),
            pltpu.SemaphoreType.DMA((n,)),
        ],
        compiler_params=params(),
        cost_estimate=cost(2 * w.size * NX * OWN + 16 * z.size, 10 * z.size + 2 * w.size + 8 * m * NX * OWN, z.size),
    )(pack([first, core] + places), labels, stats, in_hbm(z), in_hbm(r), in_hbm(w))


def own_terms(core, places, g, w):
    m, width = w.shape[1:]
    hbm, vmem = pl.BlockSpec(memory_space=pl.ANY), pl.BlockSpec(memory_space=VMEM)
    return pl.pallas_call(
        own_term_kernel,
        out_shape=term_shapes(m),
        in_specs=[pl.BlockSpec(memory_space=SMEM), hbm, hbm],
        out_specs=[vmem, vmem],
        scratch_shapes=[
            VMEM(w.shape, BF),
            VMEM((NX, width, OWN), BF),
            pltpu.SemaphoreType.DMA((NY, W_PARTS)),
            pltpu.SemaphoreType.DMA((NX,)),
        ],
        compiler_params=params(),
        cost_estimate=cost(2 * w.size * NX * OWN, 2 * w.size + g.size + 8 * m * NX * OWN),
    )(pack([core] + places), in_hbm(w), in_hbm(g))


def d_policy_kernel(x_hbm, g_hbm, out_hbm, xb, gb, ob, x_sem, g_sem, o_sem):
    tiles, _, m, _ = xb.shape

    def rows(t):
        return pl.ds(pl.multiple_of(t * m, 16), m)

    n = gb.shape[0]

    def load(t):
        return pltpu.make_async_copy(x_hbm.at[:, rows(t)], xb.at[t], x_sem.at[t])

    def store(t):
        return pltpu.make_async_copy(ob.at[t], out_hbm.at[rows(t)], o_sem.at[t])

    load_g = [pltpu.make_async_copy(g_hbm.at[b], gb.at[b], g_sem.at[b]) for b in range(n)]
    for copy in load_g:
        copy.start()
    for t in range(tiles):
        load(t).start()
    for copy in load_g:
        copy.wait()

    def step(t, _):
        load(t).wait()
        acc = 0.0
        for j in range(0, NX * NC, 2):
            lhs = jnp.concatenate((xb[t, j], xb[t, j + 1]), axis=1)
            rhs = jnp.concatenate((gb[j], gb[j + 1]), axis=1)
            acc = acc + lax.dot_general(lhs, rhs, (((1,), (1,)), ((), ())), preferred_element_type=F32)
        ob[t] = acc.astype(BF)
        store(t).start()
        return 0

    lax.fori_loop(0, tiles, step, 0)
    for t in range(tiles):
        store(t).wait()


def d_policy_of(x, g):
    n, h, _ = x.shape
    width = g.shape[1]
    tiles = 6
    m = h // tiles
    hbm = pl.BlockSpec(memory_space=pl.ANY)
    return pl.pallas_call(
        d_policy_kernel,
        out_shape=jax.ShapeDtypeStruct((h, width), BF),
        in_specs=[hbm, hbm],
        out_specs=hbm,
        scratch_shapes=[
            VMEM((tiles, n, m, OWN), BF),
            VMEM(g.shape, BF),
            VMEM((tiles, m, width), BF),
            pltpu.SemaphoreType.DMA((tiles,)),
            pltpu.SemaphoreType.DMA((n,)),
            pltpu.SemaphoreType.DMA((tiles,)),
        ],
        compiler_params=params(),
        cost_estimate=cost(2 * h * width * n * OWN, 2 * (x.size + g.size + h * width)),
    )(in_hbm(x), in_hbm(g))


UP_X, DOWN_X = by_shift(NX, 1), by_shift(NX, NX - 1)
UP_Y, DOWN_Y = by_shift(NY, 1), by_shift(NY, NY - 1)
ALL = ("x", "core", "z", "y")


def swap(a):
    return lax.ppermute(a, "core", by_xor(NC, 1))


def cut(a, first, n):
    return lax.dynamic_slice_in_dim(a, first, n, 0)


def core_route(d, second):
    pairs = []
    for x in range(NX):
        for c in range(NC):
            for z in range(NZ):
                for y in range(NY):
                    along_x = (c == 0) != second
                    x2, y2 = ((x + d) % NX, y) if along_x else (x, (y + d) % NY)
                    pairs.append((((x * NC + c) * NZ + z) * NY + y, ((x2 * NC + c) * NZ + z) * NY + y2))
    return pairs


def label_rows(ids, adv):
    top = lax.reduce_precision(adv, 8, 7)
    middle = lax.reduce_precision(adv - top, 8, 7)
    parts = [(ids >> 12).astype(F32), ((ids >> 6) & 63).astype(F32), (ids & 63).astype(F32), top, middle, adv - top - middle]
    return jnp.pad(jnp.stack(parts).astype(BF), ((0, 10), (0, 0)))


def add(a, b):
    return (a.astype(F32) + b.astype(F32)).astype(BF)


def after(value, *first):
    return lax.optimization_barrier((value, *first))[0]


def shards(hidden, ref_hidden, sampled, advantage, policy_head, ref_head):
    ix, ic, iz, iy = (lax.axis_index(a) for a in ALL)
    h, width = policy_head.shape
    half, quarter = h // 2, h // 4
    odd = iy % 2
    lo, hi, skip = odd * half, (1 - odd) * half, odd * quarter
    piece = h // (NZ * NY)
    padded = -(-piece // 16) * 16

    def block(d, other):
        return (ic ^ other) * NX + (ix + d) % NX

    own_p, own_r = hidden.T, ref_hidden.T
    marks = label_rows(sampled, advantage)
    a_p = lax.ppermute(jnp.concatenate((cut(own_p, lo, half), marks), axis=0), "x", DOWN_X)
    b_p = lax.ppermute(jnp.concatenate((cut(own_p, hi, half), marks), axis=0), "x", UP_X)
    a_r = lax.ppermute(cut(own_r, lo, half), "x", DOWN_X)
    b_r = lax.ppermute(cut(own_r, hi, half), "x", UP_X)

    wt_p, w_yz = prep(policy_head, padded)
    w_yz = w_yz.reshape(NY, NZ * padded, width)
    (wt_r,) = prep(after(ref_head, wt_p))
    a_p, b_p, wt_p, wt_r = lax.optimization_barrier((a_p, b_p, wt_p, wt_r))
    a2_p = lax.ppermute(a_p, "y", UP_Y)
    b2_p = lax.ppermute(b_p, "y", DOWN_Y)
    there = [swap(arr) for arr in (own_p, a_p, b_p)]
    a_r, b_r, *there = lax.optimization_barrier((a_r, b_r, *there))
    c = jnp.concatenate((cut(a_p, skip, quarter), cut(a_r, skip, quarter), a_p[half:]), axis=0)
    d = jnp.concatenate((cut(b_p, skip, quarter), cut(b_r, skip, quarter), b_p[half:]), axis=0)
    there += [swap(after(arr, c, d)) for arr in (a2_p, b2_p)]
    c = lax.ppermute(c, "x", DOWN_X)
    d = lax.ppermute(d, "x", UP_X)
    a2_r = lax.ppermute(a_r, "y", UP_Y)
    b2_r = lax.ppermute(b_r, "y", DOWN_Y)
    rest = quarter - skip

    def early(here, there):
        out = []
        for k, (slot, f, rows) in enumerate(((0, 0, h), (2, lo, half), (4, hi, half), (2, hi, half), (4, lo, half))):
            out += [(here[k], slot, f, rows), (there[k], slot + 1, f, rows)]
        return out

    blocks = [block(dist, s) for dist in (0, 1, 3) for s in (0, 1)]
    z, x_all = head_product(after(wt_p, c, d), early((own_p, a_p, b_p, a2_p, b2_p), there), blocks, keep=True)
    c2 = lax.ppermute(c, "y", UP_Y)
    d2 = lax.ppermute(d, "y", DOWN_Y)
    here_r = (own_r, a_r, b_r, a2_r, b2_r)
    there_r = [swap(after(arr, z, c2, d2)) for arr in here_r]
    (r,) = head_product(wt_r, early(here_r, there_r), blocks, keep=False)

    last = (c, d, c2, d2)
    last_there = [swap(arr) for arr in last]
    marks = jnp.stack((marks, a_p[half:], c[2 * quarter :], b_p[half:]))
    marks = jnp.stack((marks, jnp.stack((swap(marks[0]), there[1][half:], last_there[0][2 * quarter :], there[2][half:]))))
    marks = marks[:, :, :6].astype(F32)
    labels = jnp.stack((marks[:, :, 0] * 4096.0 + marks[:, :, 1] * 64.0 + marks[:, :, 2], marks[:, :, 3] + marks[:, :, 4] + marks[:, :, 5]), axis=2)
    labels = jnp.where(ic == 0, labels, labels[::-1])
    labels = jnp.concatenate((labels, labels), axis=1)
    labels = lax.dynamic_slice_in_dim(labels, NX - ix, NX, 1).reshape(NC * NX, 2, OWN)

    first = ((((ix * NC + ic) * NZ + iz) * NY + iy) * width).astype(I32)
    stats = row_stats(first, blocks, z, r, labels)
    late = []
    for arr, arr_there, f in zip(last, last_there, (lo + skip, hi + skip, hi + rest, lo + rest)):
        late += [(arr, 0, f, quarter), (arr_there, 1, f, quarter)]
    z, r, x_all, stats = late_product(first, labels, wt_p, wt_r, late, [block(2, s) for s in (0, 1)], z, r, x_all, stats)

    stats = all_merge(stats)
    g, far_other, near_other = grad_and_terms(first, 1 - ic, term_places(ic == 1, ix, iy), labels, stats, z, r, w_yz)
    far_mine, near_mine = own_terms(ic, term_places(ic == 0, ix, iy), g, w_yz)
    far_other = swap(far_other)
    near_other = swap(near_other)
    far = add(far_mine, far_other)
    via_up = lax.ppermute(far[:2], ALL, core_route(1, False))
    via_down = lax.ppermute(far[2:], ALL, core_route(-1, False))

    def near(k, part=slice(None)):
        return near_mine[k, part].astype(F32) + near_other[k, part].astype(F32)

    one, two = slice(0, 2), slice(2, 4)
    to_up = jnp.concatenate(((near(0, one) + via_up.astype(F32)).astype(BF), near(0, two).astype(BF)), axis=0)
    to_down = jnp.concatenate((near(1, one).astype(BF), (near(1, two) + via_down.astype(F32)).astype(BF)), axis=0)
    from_down = lax.ppermute(to_up, ALL, core_route(1, False))
    from_up = lax.ppermute(to_down, ALL, core_route(-1, False))
    d_policy = d_policy_of(x_all, after(g, to_up, to_down))
    from_down, from_up, d_policy = lax.optimization_barrier((from_down, from_up, d_policy))
    parts = near(2) + from_down.astype(F32) + from_up.astype(F32)

    at = jnp.where(ic == 0, iy, ix)
    total = lax.dynamic_index_in_dim(parts, at, 0, keepdims=False)
    parts = parts.astype(BF)
    for dist in (1, 3, 2):
        part = lax.dynamic_index_in_dim(parts, (at + dist) % NX, 0, keepdims=False)
        total = total + lax.ppermute(part, ALL, core_route(dist, True)).astype(F32)
    total = total.astype(BF).reshape(NZ, padded, OWN)
    got = lax.all_to_all(total, "z", split_axis=0, concat_axis=0, tiled=True)
    d_hidden = jnp.sum(got.astype(F32), axis=0)[:piece].T

    mine = lax.dynamic_index_in_dim(stats, block(0, 0), 0, keepdims=False)
    lse_z, _, entropy, kl = row_results(mine)
    return (mine[6] - lse_z[0], entropy[0], kl[0], d_hidden, d_policy)


def solution(mesh):
    fine = Mesh(mesh.devices.reshape(NX, NC, NZ, NY), ("x", "core", "z", "y"))
    dp, vocab = ("x", "core"), ("z", "y")
    everybody = dp + vocab
    in_specs = (P(dp, None), P(dp, None), P(dp), P(dp), P(None, everybody), P(None, everybody))
    out_specs = (P(dp), P(dp), P(dp), P(dp, vocab), P(None, everybody))
    return jax.shard_map(shards, mesh=fine, in_specs=in_specs, out_specs=out_specs, check_vma=False)
```
